128 devices in a mesh: slab: 32 (over z, y, x_lo), grid: 4 (over x_hi, core).
Axes of the slice: x: 4 (x_hi: 2, x_lo: 2; x = x_hi * 2 + x_lo), y: 4, z: 4, core: 2. Of those that a mesh axis runs over, the one named last changes fastest.
Arguments:
- eigvecs: float32 [2048, 65536], P('slab', 'grid'), may hold values from -6 to 6
- panel_one: bfloat16 [256, 65536], P('slab', 'grid'), may hold values from -0.0234375 to 0.0234375
- panel_two: bfloat16 [256, 65536], P('slab', 'grid'), may hold values from -0.0234375 to 0.0234375
- factor_one: float32 [256, 256], replicated
- factor_two: float32 [256, 256], replicated
- occupations: float32 [2048], P('slab'), may hold values from 0.3 to 3
- occupied_count: int32 [1], replicated, may hold values from 1024 to 2048
- row_offset: int32 [1], replicated, may hold values from 0 to 61440
Outputs:
- orbitals_out: float32 [2048, 65536], P('slab', 'grid')
- density: float32 [4096, 4, 16384], P('grid', None, 'slab')
The draws below stay inside these ranges and needn't reach their ends.
All inputs are finite; a program needn't handle non-finite values.
Results may differ from the reference program's by a relative error of at most 0.01.
Values may be sent and summed in bfloat16 or wider, within the bound.
No kernel may reach another device: no remote copies, remote signals or barrier semaphores. Data moves between devices by JAX's collectives and lax.ppermute only.
A program may use at most 128 MiB of HBM per device.

```python
import math
import jax
import jax.numpy as jnp
from jax import lax

N = 65536
OCC = 2048
PW = 256
R = 4096
N_GRID = 4


def draw_factor_one(key, part):
    key = jax.random.fold_in(key, 11)
    scale = 0.5 * math.sqrt(N) / PW
    upper_key, diag_key = jax.random.split(key)
    values = jax.random.normal(upper_key, (PW, PW), jnp.float32) * scale
    diagonal = jax.random.uniform(diag_key, (PW,), jnp.float32, 1.0, 2.0) * scale
    return jnp.triu(values, 1) + jnp.diag(diagonal)


def draw_factor_two(key, part):
    key = jax.random.fold_in(key, 12)
    scale = 0.5 * math.sqrt(N) / PW
    upper_key, diag_key = jax.random.split(key)
    values = jax.random.normal(upper_key, (PW, PW), jnp.float32) * scale
    diagonal = jax.random.uniform(diag_key, (PW,), jnp.float32, 1.0, 2.0) * scale
    return jnp.triu(values, 1) + jnp.diag(diagonal)


def level_of(stream_key, shape, cuts, low, high):
    def one(dim, parts):
        steps = jax.random.uniform(jax.random.fold_in(jax.random.fold_in(stream_key, 6), dim), (parts,), jnp.float32, low / len(cuts), high / len(cuts))
        return jnp.repeat(jnp.exp(steps), shape[dim] // parts).reshape((-1,) + (1,) * (len(shape) - dim - 1))

    level = one(*cuts[0])
    for cut in cuts[1:]:
        level = level * one(*cut)
    return level


def scatter_about(own_key, dims, width, most, cuts=(), held_as=jnp.bfloat16):
    factor_of = level_of(own_key, dims, cuts, -0.22, 0.18) if cuts else 1.0
    result = jax.random.normal(own_key, dims, jnp.float32) * width * factor_of
    return jnp.minimum(jnp.maximum(result, -most), most).astype(held_as)


def setup_inputs(seed: int = 0) -> dict:
    splits = jax.random.split(jax.random.key(seed), 9)
    eigvecs = scatter_about(splits[0], (OCC, N), 1.0, 6.0, ((0, 32), (1, 4)), jnp.float32)
    panel_one = scatter_about(splits[1], (PW, N), N ** -0.5, 0.0234375, ((0, 32), (1, 4)))
    panel_two = scatter_about(splits[2], (PW, N), N ** -0.5, 0.0234375, ((0, 32), (1, 4)))
    factor_one = draw_factor_one(jax.random.fold_in(splits[8], 71), 0)
    factor_two = draw_factor_two(jax.random.fold_in(splits[8], 71), 0)
    occupations = jnp.clip(jnp.exp(math.log(3.0) - 2.3025851 * jax.random.uniform(splits[5], (OCC,), jnp.float32) ** level_of(splits[5], (OCC,), ((0, 32),), -0.2, 0.2)), 0.3, 3.0)
    occupied_count = jax.random.randint(splits[6], (1,), OCC // 2, OCC + 1).astype(jnp.int32)
    row_offset = jax.random.randint(splits[7], (1,), 0, N - R + 1).astype(jnp.int32)
    return dict(eigvecs=eigvecs, panel_one=panel_one, panel_two=panel_two, factor_one=factor_one, factor_two=factor_two, occupations=occupations, occupied_count=occupied_count, row_offset=row_offset)


def apply_panel(orbs, panel, factor):
    vectors = panel.astype(jnp.float32)
    project = lax.dot_general(orbs, vectors, (((1,), (1,)), ((), ())), precision=lax.Precision.HIGHEST)
    coeffs = lax.dot_general(project, factor, (((1,), (1,)), ((), ())), precision=lax.Precision.HIGHEST)
    update = jnp.dot(coeffs, vectors, precision=lax.Precision.HIGHEST)
    return orbs - update

def reference(eigvecs, panel_one, panel_two, factor_one, factor_two, occupations, occupied_count, row_offset):
    after_one = apply_panel(eigvecs, panel_one, factor_one)
    orbitals_out = apply_panel(after_one, panel_two, factor_two)
    column = jnp.arange(OCC, dtype=jnp.int32)
    weight = jnp.where(column < occupied_count[0], occupations / math.sqrt(OCC), jnp.float32(0.0)).astype(jnp.float32)
    orbitals = orbitals_out.astype(jnp.bfloat16)
    weighted = (orbitals_out * weight[:, None]).astype(jnp.bfloat16)
    window = lax.dynamic_slice_in_dim(orbitals, row_offset[0].astype(jnp.int32), R, 1)
    full_density = lax.dot_general(window, weighted, (((0,), (0,)), ((), ())), preferred_element_type=jnp.float32)
    return (orbitals_out, full_density.reshape(R, N_GRID, N // N_GRID))
```

```python
import math

import jax
import jax.numpy as jnp
from jax import lax
from jax.sharding import Mesh
from jax.sharding import PartitionSpec as P

OCC = 2048
R = 4096
ZY = ("z", "y")
TEAM = ("z", "y", "xh", "c")


def dot(left, right, dims, **kwargs):
    return lax.dot_general(
        left, right, (dims, ((), ())), preferred_element_type=jnp.float32, **kwargs
    )


def swap(values, axis):
    return lax.ppermute(values, axis, [(0, 1), (1, 0)])


def exchange(values, axes):
    return lax.all_to_all(values, axes, 0, 0, tiled=True)


def pick(first, second, flag):
    return jnp.where(flag == 0, first, second)


def body(
    eigvecs, panel_one, panel_two, factor_one, factor_two, occupations, occupied_count, row_offset
):
    bf16 = jnp.bfloat16
    xl, xh, c = (lax.axis_index(name) for name in ("xl", "xh", "c"))
    zy = lax.axis_index(ZY)
    n_orbs, n_basis = eigvecs.shape
    n_vec = panel_one.shape[0]
    chunk = n_basis // 16
    half = chunk // 2
    pw = factor_one.shape[0]
    rows = R // 4

    vecs = jnp.concatenate([panel_one, panel_two], axis=0)
    orbs16 = eigvecs.astype(bf16)

    with jax.named_scope("window_slice"):
        both = jnp.concatenate([orbs16, vecs], axis=0)
        pad = jnp.zeros((n_orbs + 2 * n_vec, R), bf16)
        padded = jnp.concatenate([pad, both, pad], axis=1)
        start = row_offset[0] - (xh * 2 + c) * n_basis + R

        def cut(part):
            at = jnp.clip(start, 0, n_basis + R) + part * 2 * rows
            return lax.dynamic_slice_in_dim(padded, at, 2 * rows, 1)

        sent = swap(cut(1 - xh), "xh")
        kept = cut(xh)

    with jax.named_scope("vectors"):
        occ_high = occupations.astype(bf16)
        rest = occupations - occ_high.astype(jnp.float32)
        occ_mid = rest.astype(bf16)
        occ_low = (rest - occ_mid.astype(jnp.float32)).astype(bf16)
        extra = jnp.zeros((2 * n_vec, 128), bf16)
        extra = extra.at[:3, :n_orbs].set(jnp.stack([occ_high, occ_mid, occ_low]))
        packed = vecs.reshape(2 * n_vec, 16, chunk).transpose(1, 0, 2)
        packed = jnp.concatenate(
            [packed, jnp.broadcast_to(extra[None], (16, 2 * n_vec, 128))], axis=2
        )
        got = exchange(packed, ZY)
        own = got[:, :, :chunk]
        occ = got[:, :3, chunk : chunk + n_orbs].astype(jnp.float32).sum(1).reshape(16 * n_orbs)
        other = swap(own, "xl")

        def order(own, other, width):
            shape = (16, 2, n_vec, width)
            own, other = own.reshape(shape), other.reshape(shape)
            pair = jnp.stack([pick(own, other, xl), pick(other, own, xl)], axis=1)
            return pair.transpose(2, 0, 1, 3, 4).reshape(2 * pw, width)

    with jax.named_scope("window_core"):
        four = kept + sent
        four = four.reshape(n_orbs + 2 * n_vec, 2, rows)
        mine = lax.dynamic_index_in_dim(four, c, 1, keepdims=False)
        mine = mine + swap(lax.dynamic_index_in_dim(four, 1 - c, 1, keepdims=False), "c")
        mine_x = swap(mine, "xl")

    with jax.named_scope("transpose_in"):
        orbs_t = exchange(orbs16.reshape(n_orbs, 16, chunk).transpose(1, 0, 2), ZY)
        orbs_t = orbs_t.reshape(16 * n_orbs, chunk)
        vec_t = order(own, other, chunk)

    with jax.named_scope("window_gather"):
        window = lax.all_gather(jnp.stack([mine, mine_x]), ZY, axis=0)

    with jax.named_scope("project"):
        proj = dot(orbs_t, vec_t, ((1,), (1,))).astype(bf16)
        cross = dot(vec_t[:pw], vec_t[pw:], ((1,), (1,))).astype(bf16)
        n_own = 16 * n_orbs // 64
        lanes = pw * pw // (64 * n_own)
        parts = jnp.concatenate(
            [proj.reshape(64, n_own, 2 * pw), cross.reshape(64, n_own, lanes)], axis=2
        )
        summed = exchange(parts, TEAM).astype(jnp.float32).sum(0)
        high = lax.Precision.HIGHEST
        first = dot(summed[:, :pw], factor_one, ((1,), (1,)), precision=high)
        second = dot(summed[:, pw : 2 * pw], factor_two, ((1,), (1,)), precision=high)
        share = jnp.concatenate([first, second, summed[:, 2 * pw :]], axis=1).astype(bf16)
        every = exchange(jnp.broadcast_to(share[None], (64,) + share.shape), TEAM)
        cross = every[:, :, 2 * pw :].reshape(pw, pw)
        first = every[:, :, :pw].reshape(16 * n_orbs, pw)
        second = every[:, :, pw : 2 * pw].reshape(16 * n_orbs, pw)
        mixed = dot(cross.astype(jnp.float32), factor_two, ((1,), (1,)), precision=high)
        second = second.astype(jnp.float32) - dot(first, mixed.astype(bf16), ((1,), (0,)))
        coeffs = jnp.concatenate([first, second.astype(bf16)], axis=1)

    with jax.named_scope("update"):
        update = dot(coeffs, vec_t, ((1,), (0,)))
        index = (
            (jnp.arange(16, dtype=jnp.int32)[:, None] * 2 + xl) * n_orbs
            + jnp.arange(n_orbs, dtype=jnp.int32)[None]
        ).reshape(16 * n_orbs)
        weight = jnp.where(index < occupied_count[0], occ / math.sqrt(OCC), jnp.float32(0.0))
        new_t = orbs_t.astype(jnp.float32) - update
        weighted = (new_t * weight[:, None]).astype(bf16)
        update16 = update.astype(bf16)

    with jax.named_scope("spread"):
        left, right = weighted[:, :half], weighted[:, half:]
        keep, give = pick(left, right, xl), pick(right, left, xl)
        flat = ("xl", "xh")
        w_same_oth = swap(give, "xl")
        w_diff_oth = lax.ppermute(give, flat, [(i, 3 - i) for i in range(4)])
        w_diff_own = swap(keep, "xh")
        coeffs_half = lax.dynamic_slice_in_dim(coeffs, c * 8 * n_orbs, 8 * n_orbs, 0)
        coeffs_x = swap(coeffs_half, "xl")
        coeffs_y = swap(coeffs_x, "c")
        coeffs_o = jnp.concatenate(
            [pick(coeffs_x, coeffs_y, c), pick(coeffs_y, coeffs_x, c)], axis=0
        )

    with jax.named_scope("transpose_out"):
        back = exchange(update16.reshape(16, n_orbs, chunk), ZY)
        out = eigvecs - back.transpose(1, 0, 2).reshape(n_orbs, n_basis).astype(jnp.float32)

    with jax.named_scope("window_rows"):
        win_vec = order(window[:, 0, n_orbs:], window[:, 1, n_orbs:], rows)

        def rotate(piece, factors):
            piece = piece.reshape(16 * n_orbs, rows).astype(jnp.float32)
            return (piece - dot(factors, win_vec, ((1,), (0,)))).astype(bf16)

        win_own = rotate(window[:, 0, :n_orbs], coeffs)
        win_oth = rotate(window[:, 1, :n_orbs], coeffs_o)

    with jax.named_scope("density"):
        pieces = []
        for one, two in ((keep, w_same_oth), (w_diff_own, w_diff_oth)):
            one_c, two_c = swap(one, "c"), swap(two, "c")
            a = dot(win_own, one, ((0,), (0,))) + dot(win_oth, two, ((0,), (0,)))
            b = dot(win_own, one_c, ((0,), (0,))) + dot(win_oth, two_c, ((0,), (0,)))
            pieces.append((pick(a, b, c), pick(b, a, c)))
        (s0, s1), (d0, d1) = pieces
        density = jnp.stack(
            [pick(s0, d0, xh), pick(s1, d1, xh), pick(d0, s0, xh), pick(d1, s1, xh)], axis=1
        )
    return (out, density)


def solution(mesh):
    mesh = Mesh(mesh.devices.reshape(4, 4, 2, 2, 2), ("z", "y", "xl", "xh", "c"))
    slab, grid = ("z", "y", "xl"), ("xh", "c")
    both = P(slab, grid)
    in_specs = (both, both, both, P(), P(), P(slab), P(), P())
    out_specs = (both, P(grid, None, slab))
    return jax.shard_map(body, mesh=mesh, in_specs=in_specs, out_specs=out_specs, check_vma=False)
```

```python
import math

import jax
import jax.numpy as jnp
from jax import lax
from jax.experimental import pallas as pl
from jax.experimental.pallas import tpu as pltpu
from jax.sharding import Mesh
from jax.sharding import PartitionSpec as P

OCC = 2048
R = 4096
ZY = ("z", "y")
ZYC = ("z", "y", "c")
TILE = 256


def dot(left, right, dims, **kwargs):
    return lax.dot_general(
        left, right, (dims, ((), ())), preferred_element_type=jnp.float32, **kwargs
    )


def swap(values, axis):
    return lax.ppermute(values, axis, [(0, 1), (1, 0)])


def exchange(values, axes):
    return lax.all_to_all(values, axes, 0, 0, tiled=True)


def pick(first, second, flag):
    return jnp.where(flag == 0, first, second)


def body(
    eigvecs, panel_one, panel_two, factor_one, factor_two, occupations, occupied_count, row_offset
):
    bf16 = jnp.bfloat16
    xl, xh, c = (lax.axis_index(name) for name in ("xl", "xh", "c"))
    zy = lax.axis_index(ZY)
    n_orbs, n_basis = eigvecs.shape
    n_vec = panel_one.shape[0]
    chunk = n_basis // 16
    half = chunk // 2
    pw = factor_one.shape[0]
    rows = R // 4

    vecs = jnp.concatenate([panel_one, panel_two], axis=0)

    with jax.named_scope("vectors"):
        occ_high = occupations.astype(bf16)
        rest = occupations - occ_high.astype(jnp.float32)
        occ_mid = rest.astype(bf16)
        occ_low = (rest - occ_mid.astype(jnp.float32)).astype(bf16)
        extra = jnp.zeros((2 * n_vec, 128), bf16)
        extra = extra.at[:3, :n_orbs].set(jnp.stack([occ_high, occ_mid, occ_low]))
        packed = vecs.reshape(2 * n_vec, 16, chunk).transpose(1, 0, 2)
        packed = jnp.concatenate(
            [packed, jnp.broadcast_to(extra[None], (16, 2 * n_vec, 128))], axis=2
        )
        own = exchange(packed, ZY)
        other = swap(own, "xl")

        def order(own, other, width):
            shape = (16, 2, n_vec, width)
            own, other = own.reshape(shape), other.reshape(shape)
            pair = jnp.stack([pick(own, other, xl), pick(other, own, xl)], axis=1)
            return pair.transpose(2, 0, 1, 3, 4).reshape(2 * pw, width)

        def weight_of(got, side):
            occ = got[:, :3, chunk : chunk + n_orbs].astype(jnp.float32)
            occ = (occ[:, 0] + occ[:, 1]) + occ[:, 2]
            index = (jnp.arange(16, dtype=jnp.int32)[:, None] * 2 + side) * n_orbs
            index = index + jnp.arange(n_orbs, dtype=jnp.int32)[None]
            occ = jnp.where(index < occupied_count[0], occ / math.sqrt(OCC), jnp.float32(0.0))
            return occ.reshape(16 * n_orbs, 1)

        weight_own, weight_oth = weight_of(own, xl), weight_of(other, 1 - xl)
        vec_t = order(own[:, :, :chunk], other[:, :, :chunk], chunk)
        vec_half = lax.dynamic_slice_in_dim(vec_t, xl * half, half, 1)
        vec_half_x = swap(vec_half, "xh")
        vec_sides = [vec_half, swap(vec_half, "c"), vec_half_x, swap(vec_half_x, "c")]

    with jax.named_scope("window_exchange"):
        held, _ = lax.optimization_barrier((eigvecs, own))
        both = jnp.concatenate([held.astype(bf16), vecs], axis=0)
        pad = jnp.zeros((n_orbs + 2 * n_vec, R), bf16)
        padded = jnp.concatenate([pad, both, pad], axis=1)
        start = row_offset[0] - (xh * 2 + c) * n_basis + R

        def cut(part):
            at = jnp.clip(start, 0, n_basis + R) + part * 2 * rows
            return lax.dynamic_slice_in_dim(padded, at, 2 * rows, 1)

        four = cut(xh) + swap(cut(1 - xh), "xh")
        four = four.reshape(n_orbs + 2 * n_vec, 2, rows)
        mine = lax.dynamic_index_in_dim(four, c, 1, keepdims=False)
        mine = mine + swap(lax.dynamic_index_in_dim(four, 1 - c, 1, keepdims=False), "c")
        mine_x = swap(mine, "xl")

    with jax.named_scope("transpose_in"):
        orbs_t = exchange(eigvecs.astype(bf16).reshape(n_orbs, 16, chunk).transpose(1, 0, 2), ZY)
        orbs_t = orbs_t.reshape(16 * n_orbs, chunk)

    with jax.named_scope("spread"):
        left, right = orbs_t[:, :half], orbs_t[:, half:]
        keep, give = pick(left, right, xl), pick(right, left, xl)
        same_oth = swap(give, "xl")
        diff_oth = lax.ppermute(give, ("xl", "xh"), [(i, 3 - i) for i in range(4)])

    with jax.named_scope("window_gather"):
        window = lax.all_gather(jnp.stack([mine, mine_x]), ZY, axis=0)

    with jax.named_scope("project"):
        proj = dot(orbs_t, vec_t, ((1,), (1,))).astype(bf16)
        cross = dot(vec_t[:pw], vec_t[pw:], ((1,), (1,))).astype(bf16)
        n_own = 16 * n_orbs // 32
        lanes = pw * pw // (32 * n_own)
        parts = jnp.concatenate(
            [proj.reshape(32, n_own, 2 * pw), cross.reshape(32, n_own, lanes)], axis=2
        )
        summed = exchange(parts, ZYC).astype(jnp.float32).sum(0)
        summed = summed + swap(summed, "xh")

    with jax.named_scope("spread_late"):
        keep, summed = lax.optimization_barrier((keep, summed))
        diff_own = swap(keep, "xh")
        sides = [(keep, same_oth), None, (diff_own, diff_oth), None]
        sides[1] = tuple(swap(part, "c") for part in sides[0])
        sides[3] = tuple(swap(part, "c") for part in sides[2])

    with jax.named_scope("coefficients"):
        high = lax.Precision.HIGHEST
        first = dot(summed[:, :pw], factor_one, ((1,), (1,)), precision=high)
        second = dot(summed[:, pw : 2 * pw], factor_two, ((1,), (1,)), precision=high)
        share = jnp.concatenate([first, second, summed[:, 2 * pw :]], axis=1).astype(bf16)
        every = exchange(jnp.broadcast_to(share[None], (32,) + share.shape), ZYC)
        cross = every[:, :, 2 * pw :].reshape(pw, pw)
        first = every[:, :, :pw].reshape(16 * n_orbs, pw)
        second = every[:, :, pw : 2 * pw].reshape(16 * n_orbs, pw)
        mixed = dot(cross.astype(jnp.float32), factor_two, ((1,), (1,)), precision=high)
        second = second.astype(jnp.float32) - dot(first, mixed.astype(bf16), ((1,), (0,)))
        coeffs = jnp.concatenate([first, second.astype(bf16)], axis=1)
        coeffs_half = lax.dynamic_slice_in_dim(coeffs, c * 8 * n_orbs, 8 * n_orbs, 0)
        coeffs_x = swap(coeffs_half, "xl")
        coeffs_y = swap(coeffs_x, "c")
        coeffs_o = jnp.concatenate(
            [pick(coeffs_x, coeffs_y, c), pick(coeffs_y, coeffs_x, c)], axis=0
        )

    with jax.named_scope("transpose_out"):
        update = dot(coeffs, vec_t, ((1,), (0,))).astype(bf16)
        back = exchange(update.reshape(16, n_orbs, chunk), ZY)
        out = eigvecs - back.transpose(1, 0, 2).reshape(n_orbs, n_basis).astype(jnp.float32)

    with jax.named_scope("window_rows"):
        win_vec = order(window[:, 0, n_orbs:], window[:, 1, n_orbs:], rows)

        def rotate(piece, factors):
            piece = piece.reshape(16 * n_orbs, rows).T.astype(jnp.float32)
            return (piece - dot(win_vec, factors, ((0,), (1,)))).astype(bf16)

        win_own = rotate(window[:, 0, :n_orbs], coeffs)
        win_oth = rotate(window[:, 1, :n_orbs], coeffs_o)

    with jax.named_scope("density"):
        place = (xh * 2 + c).astype(jnp.int32).reshape(1)
        density = density_of(
            place, win_own, win_oth, coeffs, coeffs_o, weight_own, weight_oth, sides, vec_sides
        )
    return (out, density)


def density_kernel(place, win_own, win_oth, coeffs, coeffs_o, weight_own, weight_oth, *rest):
    orbs, vecs, out, weighted = rest[:8], rest[8:12], rest[12], rest[13]
    n_half = coeffs.shape[0]

    @pl.when(pl.program_id(0) == 0)
    def _():
        for side in range(4):
            for part, (factor, weight) in enumerate(
                ((coeffs, weight_own), (coeffs_o, weight_oth))
            ):

                @pl.loop(0, n_half // TILE)
                def _(step):
                    at = pl.ds(pl.multiple_of(step * TILE, TILE), TILE)
                    update = dot(factor[at, :], vecs[side][...], ((1,), (0,)))
                    new = orbs[2 * side + part][at, :].astype(jnp.float32) - update
                    new = (new * weight[at, :]).astype(jnp.bfloat16)
                    to = pl.ds(pl.multiple_of(part * n_half + step * TILE, TILE), TILE)
                    weighted[side, to, :] = new

    for block in range(4):
        side = jnp.bitwise_xor(place[0], block)
        total = dot(win_own[...], weighted[side, :n_half, :], ((1,), (0,)))
        total = total + dot(win_oth[...], weighted[side, n_half:, :], ((1,), (0,)))
        out[:, block, :] = total


def density_of(place, win_own, win_oth, coeffs, coeffs_o, weight_own, weight_oth, sides, vecs):
    rows, n_half = win_own.shape
    width = vecs[0].shape[1]
    operands = [coeffs, coeffs_o, weight_own, weight_oth]
    operands += [part for side in sides for part in side] + list(vecs)
    whole = [
        pl.BlockSpec(value.shape, lambda i, _: (0, 0), pipeline_mode=pl.Buffered(1))
        for value in operands
    ]
    tile = pl.BlockSpec((TILE, n_half), lambda i, _: (i, 0))
    return pl.pallas_call(
        density_kernel,
        out_shape=jax.ShapeDtypeStruct((rows, 4, width), jnp.float32),
        grid_spec=pltpu.PrefetchScalarGridSpec(
            num_scalar_prefetch=1,
            grid=(rows // TILE,),
            in_specs=[tile, tile] + whole,
            out_specs=pl.BlockSpec((TILE, 4, width), lambda i, _: (i, 0, 0)),
            scratch_shapes=[pltpu.VMEM((4, 2 * n_half, width), jnp.bfloat16)],
        ),
        compiler_params=pltpu.CompilerParams(vmem_limit_bytes=48 * 2**20),
        cost_estimate=pl.CostEstimate(
            flops=2 * rows * 2 * n_half * 4 * width + 16 * n_half * 512 * width,
            bytes_accessed=28 * 2**20,
            transcendentals=0,
        ),
        name="density",
    )(place, win_own, win_oth, *operands)


def solution(mesh):
    mesh = Mesh(mesh.devices.reshape(4, 4, 2, 2, 2), ("z", "y", "xl", "xh", "c"))
    slab, grid = ("z", "y", "xl"), ("xh", "c")
    both = P(slab, grid)
    in_specs = (both, both, both, P(), P(), P(slab), P(), P())
    out_specs = (both, P(grid, None, slab))
    return jax.shard_map(body, mesh=mesh, in_specs=in_specs, out_specs=out_specs, check_vma=False)
```

```python
import functools
import math

import jax
import jax.numpy as jnp
from jax import lax
from jax.experimental import pallas as pl
from jax.experimental.pallas import tpu as pltpu
from jax.sharding import Mesh
from jax.sharding import PartitionSpec as P

OCC = 2048
R = 4096
ZY = ("z", "y")
ZYC = ("z", "y", "c")
TILE = 256


def dot(left, right, dims, **kwargs):
    return lax.dot_general(
        left, right, (dims, ((), ())), preferred_element_type=jnp.float32, **kwargs
    )


def swap(values, axis):
    return lax.ppermute(values, axis, [(0, 1), (1, 0)])


def exchange(values, axes):
    return lax.all_to_all(values, axes, 0, 0, tiled=True)


def tie(*values):
    return lax.optimization_barrier(values)


def pick(first, second, flag):
    return jnp.where(flag == 0, first, second)


def body(
    eigvecs, panel_one, panel_two, factor_one, factor_two, occupations, occupied_count, row_offset
):
    bf16 = jnp.bfloat16
    xl, xh, c = (lax.axis_index(name) for name in ("xl", "xh", "c"))
    zy = lax.axis_index(ZY)
    n_orbs, n_basis = eigvecs.shape
    n_vec = panel_one.shape[0]
    chunk = n_basis // 16
    half = chunk // 2
    pw = factor_one.shape[0]
    rows = R // 4

    n_all = 2 * n_vec
    side_xl = xl.astype(jnp.int32).reshape(1)
    place = jnp.stack([xh * 2 + c, c]).astype(jnp.int32)

    with jax.named_scope("pack"):
        occ_high = occupations.astype(bf16)
        rest = occupations - occ_high.astype(jnp.float32)
        occ_mid = rest.astype(bf16)
        occ_low = (rest - occ_mid.astype(jnp.float32)).astype(bf16)
        extra = jnp.zeros((16, half), bf16)
        extra = extra.at[:3, :n_orbs].set(jnp.stack([occ_high, occ_mid, occ_low]))
        give_p, keep_p = pack(side_xl, eigvecs, panel_one, panel_two, extra, chunk)

    with jax.named_scope("transpose_give"):
        got = exchange(give_p, ZY)

    with jax.named_scope("window_exchange"):
        start = row_offset[0] - (xh * 2 + c) * n_basis
        held, _ = tie(eigvecs, give_p)

        def cut(part):
            first = start + part * rows
            at = jnp.clip(first, 0, n_basis - rows)
            pieces = (held, panel_one, panel_two)
            pieces = [lax.dynamic_slice_in_dim(v, at, rows, 1).astype(bf16) for v in pieces]
            piece = jnp.concatenate(pieces)
            zeros = jnp.zeros_like(piece)
            piece = jnp.concatenate([zeros, piece, zeros], axis=1)
            shift = jnp.clip(first - at, -rows, rows)
            return lax.dynamic_slice_in_dim(piece, rows + shift, rows, 1)

        both_flip = [(i, 3 - i) for i in range(4)]
        from_xh = swap(cut((1 - xh) * 2 + c), "xh")
        from_both = lax.ppermute(cut((1 - xh) * 2 + 1 - c), ("xh", "c"), both_flip)
        from_c = swap(cut(xh * 2 + 1 - c), "c")
        mine = (cut(xh * 2 + c) + from_c) + (from_xh + from_both)
        mine_x = swap(mine, "xl")

        def by_xl(own, other, axis):
            return jnp.stack([pick(own, other, xl), pick(other, own, xl)], axis=axis)

        win_vecs = by_xl(mine[n_orbs:], mine_x[n_orbs:], 0).reshape(2 * n_all, rows)
        window = jnp.concatenate([mine[:n_orbs], mine_x[:n_orbs], win_vecs], axis=0)
        got, keep_p, window = tie(got, keep_p, window)
        window = lax.all_gather(window, ZY, axis=0)

    with jax.named_scope("transpose_keep"):
        keep = exchange(keep_p, ZY)
        give = got[:, :n_orbs].reshape(16 * n_orbs, half)
        vec_own = got[:, n_orbs : n_orbs + 2 * n_all]
        occ_own = got[:, n_orbs + 2 * n_all :, :128]
        vec_oth = swap(vec_own, "xl")
        occ_oth = swap(occ_own, "xl")
        quarter = 8 * n_orbs
        give_a, give_b = give[:quarter], give[quarter:]
        same_a = swap(give_a, "xl")
        diff_a = lax.ppermute(give_a, ("xl", "xh"), both_flip)
        count, factor_one, factor_two, vec_oth = tie(
            occupied_count, factor_one, factor_two, vec_oth
        )

        def weight_of(occ, side):
            occ = occ[:, :3, :n_orbs].astype(jnp.float32)
            occ = (occ[:, 0] + occ[:, 1]) + occ[:, 2]
            index = (jnp.arange(16, dtype=jnp.int32)[:, None] * 2 + side) * n_orbs
            index = index + jnp.arange(n_orbs, dtype=jnp.int32)[None]
            occ = jnp.where(index < count[0], occ / math.sqrt(OCC), jnp.float32(0.0))
            return occ.reshape(16 * n_orbs, 1)

        weight_own, weight_oth = weight_of(occ_own, xl), weight_of(occ_oth, 1 - xl)
        vecs = by_xl(vec_own.reshape(16, 2, n_all, half), vec_oth.reshape(16, 2, n_all, half), 2)
        vecs = vecs.transpose(1, 0, 2, 3, 4)
        vec_two = vecs.reshape(2, 32, 2, n_vec, half)[:, :, 1].reshape(2, pw, half)
        vecs = vecs.reshape(2, 2 * pw, half)
        vec_keep = lax.dynamic_index_in_dim(vecs, xl, 0, keepdims=False)
        vec_give = lax.dynamic_index_in_dim(vecs, 1 - xl, 0, keepdims=False)

        high = lax.Precision.HIGHEST
        at_v = jnp.arange(pw, dtype=jnp.int32)[:, None]
        at_q = jnp.arange(2 * pw, dtype=jnp.int32)[None]
        factor = jnp.zeros((2 * pw, 2 * pw), jnp.float32)
        for panel, one in enumerate((factor_one, factor_two)):
            spot = (at_v // n_vec) * 2 * n_vec + panel * n_vec + at_v % n_vec
            place_of = (at_q == spot).astype(jnp.float32)
            wide = dot(one, place_of, ((0,), (0,)), precision=high)
            factor = factor + dot(place_of, wide, ((0,), (0,)), precision=high)
        wide_high = wide.astype(bf16)
        wide_low = (wide - wide_high.astype(jnp.float32)).astype(bf16)
        vec_keep_x = lax.ppermute(vec_give, ("xl", "xh"), both_flip)
        keep, same_a, diff_a, vecs, vec_two, vec_keep = tie(
            keep, same_a, diff_a, vecs, vec_two, vec_keep
        )
        keep, weight_own, weight_oth, factor, wide_high, wide_low = tie(
            keep, weight_own, weight_oth, factor, wide_high, wide_low
        )
        keep = keep.reshape(16 * n_orbs, half)

    with jax.named_scope("project"):
        cross_a = swap(keep[:quarter], "xh")
        parts = project(side_xl, give, keep, vecs, vec_two)
        summed = exchange(parts, ZYC)
        keep_c, same_a_c, diff_a_c, vec_keep_c = (
            swap(v, "c") for v in (keep, same_a, diff_a, vec_keep)
        )
        summed, cross_a, keep_c, same_a_c, diff_a_c, vec_keep_c, vec_keep_x = tie(
            summed, cross_a, keep_c, same_a_c, diff_a_c, vec_keep_c, vec_keep_x
        )
        summed = summed.astype(jnp.float32).sum(0)
        summed = summed + swap(summed, "xh")
        summed, late = tie(summed, keep)

    with jax.named_scope("coefficients"):
        share = dot(summed[:, : 2 * pw], factor, ((1,), (0,)), precision=high)
        share = jnp.concatenate([share, summed[:, 2 * pw :]], axis=1).astype(bf16)
        every = exchange(jnp.broadcast_to(share[None], (32,) + share.shape), ZYC)
        cross_b = swap(late[quarter:], "xh")
        cross_a_c, vec_keep_xc = swap(cross_a, "c"), swap(vec_keep_x, "c")
        every, cross_b, cross_a_c, vec_keep_xc, give_b = tie(
            every, cross_b, cross_a_c, vec_keep_xc, give_b
        )
        coeffs, coeffs_half, update = expand(place, every, wide_high, wide_low, vecs, n_orbs)

    with jax.named_scope("transpose_out"):
        back = exchange(update, ZY)

    with jax.named_scope("density"):
        coeffs_x = swap(coeffs_half, "xl")
        cross_b_c = swap(cross_b, "c")
        give_b, coeffs_half = tie(give_b, coeffs_half)
        same_b = swap(give_b, "xl")
        diff_b = lax.ppermute(give_b, ("xl", "xh"), both_flip)
        vec_sides = [vec_keep, vec_keep_c, vec_keep_x, vec_keep_xc]
        first = density_part(
            0,
            place,
            window,
            [coeffs],
            weight_own,
            [[keep], [keep_c], [cross_a, cross_b], [cross_a_c, cross_b_c]],
            vec_sides,
        )
        first, coeffs_x, same_b, diff_b = tie(first, coeffs_x, same_b, diff_b)
        coeffs_y = swap(coeffs_x, "c")
        same_b_c, diff_b_c = swap(same_b, "c"), swap(diff_b, "c")
        density = density_part(
            1,
            place,
            window,
            [coeffs_x, coeffs_y],
            weight_oth,
            [[same_a, same_b], [same_a_c, same_b_c], [diff_a, diff_b], [diff_a_c, diff_b_c]],
            vec_sides,
            first,
        )

    with jax.named_scope("subtract"):
        back, density = tie(back, density)
        out = subtract(eigvecs, back)
    return (out, density)


def cost(flops, bytes_accessed):
    return pl.CostEstimate(flops=flops, bytes_accessed=bytes_accessed, transcendentals=0)


def pack_kernel(side, orbs, panel_one, panel_two, extra, give, keep):
    parts, n_orbs, half = keep.shape
    n_all = 2 * panel_one.shape[0]
    vecs = jnp.concatenate([panel_one[...], panel_two[...]], axis=0)
    for part in range(parts):
        for out, which in ((keep, side[0]), (give, 1 - side[0])):
            at = pl.multiple_of((2 * part + which) * half, half)
            out[part, :n_orbs, :] = orbs[:, pl.ds(at, half)].astype(jnp.bfloat16)
        for which in range(2):
            at = (2 * part + which) * half
            rows = pl.ds(n_orbs + which * n_all, n_all)
            give[part, rows, :] = vecs[:, at : at + half]
        give[part, pl.ds(n_orbs + 2 * n_all, 16), :] = extra[...]


def pack(side, orbs, panel_one, panel_two, extra, chunk):
    n_orbs, n_basis = orbs.shape
    n_vec = panel_one.shape[0]
    parts, half = n_basis // chunk, chunk // 2
    step = 4

    def split(value):
        return pl.BlockSpec((value.shape[0], step * chunk), lambda i, _: (0, i))

    n_give = n_orbs + 4 * n_vec + 16
    return pl.pallas_call(
        pack_kernel,
        out_shape=(
            jax.ShapeDtypeStruct((parts, n_give, half), jnp.bfloat16),
            jax.ShapeDtypeStruct((parts, n_orbs, half), jnp.bfloat16),
        ),
        grid_spec=pltpu.PrefetchScalarGridSpec(
            num_scalar_prefetch=1,
            grid=(parts // step,),
            in_specs=[split(orbs), split(panel_one), split(panel_two)]
            + [pl.BlockSpec(extra.shape, lambda i, _: (0, 0))],
            out_specs=(
                pl.BlockSpec((step, n_give, half), lambda i, _: (i, 0, 0)),
                pl.BlockSpec((step, n_orbs, half), lambda i, _: (i, 0, 0)),
            ),
        ),
        compiler_params=pltpu.CompilerParams(vmem_limit_bytes=60 * 2**20),
        cost_estimate=cost(0, 7 * n_orbs * n_basis),
        name="pack",
    )(side, orbs, panel_one, panel_two, extra)


def subtract_kernel(orbs, update, out):
    parts, _, chunk = update.shape
    for part in range(parts):
        at = pl.ds(part * chunk, chunk)
        out[:, at] = orbs[:, at] - update[part].astype(jnp.float32)


def subtract(orbs, update):
    n_orbs, n_basis = orbs.shape
    parts, _, chunk = update.shape
    step = 4
    block = pl.BlockSpec((n_orbs, step * chunk), lambda i: (0, i))
    return pl.pallas_call(
        subtract_kernel,
        out_shape=jax.ShapeDtypeStruct(orbs.shape, jnp.float32),
        grid=(parts // step,),
        in_specs=[block, pl.BlockSpec((step, n_orbs, chunk), lambda i: (i, 0, 0))],
        out_specs=block,
        compiler_params=pltpu.CompilerParams(vmem_limit_bytes=60 * 2**20),
        cost_estimate=cost(n_orbs * n_basis, 10 * n_orbs * n_basis),
        name="subtract_update",
    )(orbs, update)


def project_kernel(side, give, keep, vecs, vec_two, out):
    blocks, n_own, lanes = out.shape
    width = vecs.shape[1]
    proj = dot(give[...], vecs[1 - side[0]], ((1,), (1,)))
    proj = proj + dot(keep[...], vecs[side[0]], ((1,), (1,)))
    out[:, :, :width] = proj.astype(jnp.bfloat16).reshape(blocks, n_own, width)
    cross = dot(vecs[0], vec_two[0], ((1,), (1,)))
    cross = cross + dot(vecs[1], vec_two[1], ((1,), (1,)))
    out[:, :, width:] = cross.astype(jnp.bfloat16).reshape(blocks, n_own, lanes - width)


def project(side, give, keep, vecs, vec_two):
    n_orbs, half = give.shape
    width, n_two = vecs.shape[1], vec_two.shape[1]
    tile, lanes = n_orbs // 2, n_two // 2
    return pl.pallas_call(
        project_kernel,
        out_shape=jax.ShapeDtypeStruct((32, n_orbs // 32, width + lanes), jnp.bfloat16),
        grid_spec=pltpu.PrefetchScalarGridSpec(
            num_scalar_prefetch=1,
            grid=(2,),
            in_specs=[
                pl.BlockSpec((tile, half), lambda i, _: (i, 0)),
                pl.BlockSpec((tile, half), lambda i, _: (i, 0)),
                pl.BlockSpec(vecs.shape, lambda i, _: (0, 0, 0)),
                pl.BlockSpec((2, lanes, half), lambda i, _: (0, i, 0)),
            ],
            out_specs=pl.BlockSpec((16, n_orbs // 32, width + lanes), lambda i, _: (i, 0, 0)),
        ),
        compiler_params=pltpu.CompilerParams(vmem_limit_bytes=18 * 2**20),
        cost_estimate=cost(4 * n_orbs * width * half, 6 * 2**20),
        name="project",
    )(side, give, keep, vecs, vec_two)


def expand_kernel(place, every, wide_high, wide_low, vecs, coeffs, mine, update, mixed):
    width, half = vecs.shape[1:]
    step = pl.program_id(0)
    blocks, n_own = every.shape[0] // 2, every.shape[1]

    @pl.when(step == 0)
    def _():
        lanes = every.shape[2] - width
        total = None
        for part in range(2):
            cross = every[part * blocks : (part + 1) * blocks, :, width:].reshape(width, lanes)
            at = pl.ds(part * lanes, lanes)
            for wide in (wide_high, wide_low):
                term = dot(cross, wide[at, :], ((1,), (0,)))
                total = term if total is None else total + term
        row = lax.broadcasted_iota(jnp.int32, total.shape, 0)
        first = jnp.bitwise_and(lax.shift_right_logical(row, 3), 1) == 0
        mixed[...] = jnp.where(first, total, 0.0).astype(jnp.bfloat16)

    base = every[pl.ds(step * blocks, blocks), :, :width].reshape(blocks * n_own, width)
    fixed = base.astype(jnp.float32) - dot(base, mixed[...], ((1,), (0,)))
    fixed = fixed.astype(jnp.bfloat16)
    coeffs[...] = fixed

    @pl.when(step == place[1])
    def _():
        mine[...] = fixed

    for part in range(2):
        new = dot(fixed, vecs[part], ((1,), (0,))).astype(jnp.bfloat16)
        update[:, :, part * half : (part + 1) * half] = new.reshape(update.shape[:2] + (half,))


def expand(place, every, wide_high, wide_low, vecs, n_orbs):
    _, width, half = vecs.shape
    total = every.shape[0] * every.shape[1]

    def whole(value):
        zeros = (0,) * value.ndim
        return pl.BlockSpec(value.shape, lambda i, _: zeros, pipeline_mode=pl.Buffered(1))

    return pl.pallas_call(
        expand_kernel,
        out_shape=(
            jax.ShapeDtypeStruct((total, width), jnp.bfloat16),
            jax.ShapeDtypeStruct((total // 2, width), jnp.bfloat16),
            jax.ShapeDtypeStruct((16, n_orbs, 2 * half), jnp.bfloat16),
        ),
        grid_spec=pltpu.PrefetchScalarGridSpec(
            num_scalar_prefetch=1,
            grid=(2,),
            in_specs=[whole(value) for value in (every, wide_high, wide_low, vecs)],
            out_specs=(
                pl.BlockSpec((total // 2, width), lambda i, _: (i, 0)),
                pl.BlockSpec((total // 2, width), lambda i, _: (0, 0)),
                pl.BlockSpec((8, n_orbs, 2 * half), lambda i, _: (i, 0, 0)),
            ),
            scratch_shapes=[pltpu.VMEM((width, width), jnp.bfloat16)],
        ),
        compiler_params=pltpu.CompilerParams(vmem_limit_bytes=18 * 2**20),
        cost_estimate=cost(2 * total * width * (width + 2 * half), 6 * 2**20),
        name="expand",
    )(place, every, wide_high, wide_low, vecs)


def density_kernel(n_factors, counts, place, win_orbs, win_vecs, *refs):
    factors, refs = refs[:n_factors], refs[n_factors:]
    weight, refs = refs[0], refs[1:]
    orbs = []
    for n in counts:
        orbs.append(refs[:n])
        refs = refs[n:]
    vecs, refs = refs[:4], refs[4:]
    so_far = refs[0] if n_factors == 2 else None
    out, weighted, coeffs = refs[-3:]
    n_half, width = coeffs.shape
    tile = win_orbs.shape[2]

    @pl.when(pl.program_id(0) == 0)
    def _():
        if n_factors == 1:
            coeffs[...] = factors[0][...]
        else:
            for core, factor in ((place[1], factors[0]), (1 - place[1], factors[1])):
                to = pl.multiple_of(core * (n_half // 2), n_half // 2)
                coeffs[pl.ds(to, n_half // 2), :] = factor[...]
        for side in range(4):
            rows = n_half // len(orbs[side])
            for i, piece in enumerate(orbs[side]):
                at = pl.ds(i * rows, rows)
                update = dot(coeffs[at, :], vecs[side][...], ((1,), (0,)))
                new = piece[...].astype(jnp.float32) - update
                weighted[side, at, :] = (new * weight[at, :]).astype(jnp.bfloat16)

    update = dot(coeffs[...], win_vecs[...].reshape(width, tile), ((1,), (0,)))
    turned = win_orbs[...].reshape(n_half, tile).astype(jnp.float32) - update
    turned = turned.astype(jnp.bfloat16).T
    for block in range(4):
        side = jnp.bitwise_xor(place[0], block)
        total = dot(turned, weighted[side], ((1,), (0,)))
        if so_far is not None:
            total = total + so_far[:, block, :]
        out[:, block, :] = total


def density_part(part, place, window, factors, weight, orbs, vecs, so_far=None):
    rows = window.shape[2]
    n_half, width = weight.shape[0], vecs[0].shape[1]
    n_vec, n_orbs = vecs[0].shape[0] // 16, n_half // 16
    flat = [piece for side in orbs for piece in side]
    operands = [*factors, weight, *flat, *vecs]
    specs = [
        pl.BlockSpec((16, n_orbs, TILE), lambda i, _: (0, part, i)),
        pl.BlockSpec((16, n_vec, TILE), lambda i, _: (0, 2 * n_orbs // n_vec, i)),
    ]
    specs += [
        pl.BlockSpec(value.shape, lambda i, _: (0, 0), pipeline_mode=pl.Buffered(1))
        for value in operands
    ]
    block = pl.BlockSpec((TILE, 4, width), lambda i, _: (i, 0, 0))
    aliases = {}
    if so_far is not None:
        specs.append(block)
        operands.append(so_far)
        aliases = {2 + len(operands): 0}
    kernel = functools.partial(density_kernel, len(factors), [len(side) for side in orbs])
    return pl.pallas_call(
        kernel,
        out_shape=jax.ShapeDtypeStruct((rows, 4, width), jnp.float32),
        grid_spec=pltpu.PrefetchScalarGridSpec(
            num_scalar_prefetch=1,
            grid=(rows // TILE,),
            in_specs=specs,
            out_specs=block,
            scratch_shapes=[
                pltpu.VMEM((4, n_half, width), jnp.bfloat16),
                pltpu.VMEM((n_half, vecs[0].shape[0]), jnp.bfloat16),
            ],
        ),
        input_output_aliases=aliases,
        compiler_params=pltpu.CompilerParams(vmem_limit_bytes=60 * 2**20),
        cost_estimate=cost(2 * rows * n_half * (4 * width + 1024), 20 * 2**20),
        name="density_own" if part == 0 else "density_other",
    )(place, window, window, *operands)


def solution(mesh):
    mesh = Mesh(mesh.devices.reshape(4, 4, 2, 2, 2), ("z", "y", "xl", "xh", "c"))
    slab, grid = ("z", "y", "xl"), ("xh", "c")
    both = P(slab, grid)
    in_specs = (both, both, both, P(), P(), P(slab), P(), P())
    out_specs = (both, P(grid, None, slab))
    return jax.shard_map(body, mesh=mesh, in_specs=in_specs, out_specs=out_specs, check_vma=False)
```

```python
import functools
import math

import jax
import jax.numpy as jnp
from jax import lax
from jax.experimental import pallas as pl
from jax.experimental.pallas import tpu as pltpu
from jax.sharding import Mesh
from jax.sharding import PartitionSpec as P

OCC = 2048
R = 4096
ZY = ("z", "y")
ZYC = ("z", "y", "c")
TILE = 256
STEPS = 8


def dot(left, right, dims, **kwargs):
    return lax.dot_general(
        left, right, (dims, ((), ())), preferred_element_type=jnp.float32, **kwargs
    )


def swap(values, axis):
    return lax.ppermute(values, axis, [(0, 1), (1, 0)])


def exchange(values, axes):
    return lax.all_to_all(values, axes, 0, 0, tiled=True)


def tie(*values):
    return lax.optimization_barrier(values)


def pick(first, second, flag):
    return jnp.where(flag == 0, first, second)


def body(
    eigvecs, panel_one, panel_two, factor_one, factor_two, occupations, occupied_count, row_offset
):
    bf16 = jnp.bfloat16
    xl, xh, c = (lax.axis_index(name) for name in ("xl", "xh", "c"))
    zy = lax.axis_index(ZY)
    n_orbs, n_basis = eigvecs.shape
    n_vec = panel_one.shape[0]
    chunk = n_basis // 16
    half = chunk // 2
    pw = factor_one.shape[0]
    rows = R // 4

    n_all = 2 * n_vec
    side_xl = xl.astype(jnp.int32).reshape(1)
    place = jnp.stack([xh * 2 + c, c]).astype(jnp.int32)

    with jax.named_scope("pack"):
        occ_high = occupations.astype(bf16)
        rest = occupations - occ_high.astype(jnp.float32)
        occ_mid = rest.astype(bf16)
        occ_low = (rest - occ_mid.astype(jnp.float32)).astype(bf16)
        extra = jnp.zeros((16, half), bf16)
        extra = extra.at[:3, :n_orbs].set(jnp.stack([occ_high, occ_mid, occ_low]))
        give_p, keep_p = pack(side_xl, eigvecs, panel_one, panel_two, extra, chunk)

    with jax.named_scope("transpose_give"):
        got = exchange(give_p, ZY)

    with jax.named_scope("window_exchange"):
        start = row_offset[0] - (xh * 2 + c) * n_basis
        held, _ = tie(eigvecs, give_p)

        def cut(part):
            first = start + part * rows
            at = jnp.clip(first, 0, n_basis - rows)
            pieces = (held, panel_one, panel_two)
            pieces = [lax.dynamic_slice_in_dim(v, at, rows, 1).astype(bf16) for v in pieces]
            piece = jnp.concatenate(pieces)
            zeros = jnp.zeros_like(piece)
            piece = jnp.concatenate([zeros, piece, zeros], axis=1)
            shift = jnp.clip(first - at, -rows, rows)
            return lax.dynamic_slice_in_dim(piece, rows + shift, rows, 1)

        both_flip = [(i, 3 - i) for i in range(4)]
        from_xh = swap(cut((1 - xh) * 2 + c), "xh")
        from_both = lax.ppermute(cut((1 - xh) * 2 + 1 - c), ("xh", "c"), both_flip)
        from_c = swap(cut(xh * 2 + 1 - c), "c")
        mine = (cut(xh * 2 + c) + from_c) + (from_xh + from_both)
        mine_x = swap(mine, "xl")

        def by_xl(own, other, axis):
            return jnp.stack([pick(own, other, xl), pick(other, own, xl)], axis=axis)

        win_vecs = by_xl(mine[n_orbs:], mine_x[n_orbs:], 0).reshape(2 * n_all, rows)
        window = jnp.concatenate([mine[:n_orbs], mine_x[:n_orbs], win_vecs], axis=0)
        got, keep_p, window = tie(got, keep_p, window)
        window = lax.all_gather(window, ZY, axis=0)

    with jax.named_scope("transpose_keep"):
        keep = exchange(keep_p, ZY)
        give = got[:, :n_orbs].reshape(16 * n_orbs, half)
        vec_own = got[:, n_orbs : n_orbs + 2 * n_all]
        occ_own = got[:, n_orbs + 2 * n_all :, :128]
        vec_oth = swap(vec_own, "xl")
        occ_oth = swap(occ_own, "xl")
        quarter = 8 * n_orbs
        count, factor_one, factor_two, give, occ_oth = tie(
            occupied_count, factor_one, factor_two, give, occ_oth
        )
        give_a, give_b = give[:quarter], give[quarter:]
        same_a = swap(give_a, "xl")
        diff_a = lax.ppermute(give_a, ("xl", "xh"), both_flip)

        def weight_of(occ, side):
            occ = occ[:, :3, :n_orbs].astype(jnp.float32)
            occ = (occ[:, 0] + occ[:, 1]) + occ[:, 2]
            index = (jnp.arange(16, dtype=jnp.int32)[:, None] * 2 + side) * n_orbs
            index = index + jnp.arange(n_orbs, dtype=jnp.int32)[None]
            occ = jnp.where(index < count[0], occ / math.sqrt(OCC), jnp.float32(0.0))
            return occ.reshape(16 * n_orbs, 1)

        weight_own, weight_oth = weight_of(occ_own, xl), weight_of(occ_oth, 1 - xl)
        vecs = by_xl(vec_own.reshape(16, 2, n_all, half), vec_oth.reshape(16, 2, n_all, half), 2)
        vecs = vecs.transpose(1, 0, 2, 3, 4)
        vec_two = vecs.reshape(2, 32, 2, n_vec, half)[:, :, 1].reshape(2, pw, half)
        vecs = vecs.reshape(2, 2 * pw, half)
        vec_keep = lax.dynamic_index_in_dim(vecs, xl, 0, keepdims=False)
        vec_give = lax.dynamic_index_in_dim(vecs, 1 - xl, 0, keepdims=False)

        high = lax.Precision.HIGHEST
        at_v = jnp.arange(pw, dtype=jnp.int32)[:, None]
        at_q = jnp.arange(2 * pw, dtype=jnp.int32)[None]
        factor = jnp.zeros((2 * pw, 2 * pw), jnp.float32)
        for panel, one in enumerate((factor_one, factor_two)):
            spot = (at_v // n_vec) * 2 * n_vec + panel * n_vec + at_v % n_vec
            place_of = (at_q == spot).astype(jnp.float32)
            wide = dot(one, place_of, ((0,), (0,)), precision=high)
            factor = factor + dot(place_of, wide, ((0,), (0,)), precision=high)
        wide_high = wide.astype(bf16)
        wide_low = (wide - wide_high.astype(jnp.float32)).astype(bf16)
        vec_keep_c = swap(vec_keep, "c")
        keep, same_a, diff_a, vecs, vec_two, vec_keep = tie(
            keep, same_a, diff_a, vecs, vec_two, vec_keep
        )
        keep, vec_keep_c = tie(keep, vec_keep_c)
        keep, weight_own, weight_oth, factor, wide_high, wide_low = tie(
            keep, weight_own, weight_oth, factor, wide_high, wide_low
        )
        keep = keep.reshape(16 * n_orbs, half)

    with jax.named_scope("project"):
        cross = swap(keep, "xh")
        parts, parts_c = project(side_xl, place, give, keep, vecs, vec_two)
        parts = parts.astype(jnp.float32) + swap(parts_c, "c").astype(jnp.float32)
        summed = exchange(parts.astype(bf16), ZY)
        summed, cross = tie(summed, cross)
        summed = summed.astype(jnp.float32).sum(0)
        summed = summed + swap(summed, "xh")
        summed, give_b = tie(summed, give_b)

    with jax.named_scope("coefficients"):
        share = dot(summed[:, : 2 * pw], factor, ((1,), (0,)), precision=high)
        share = jnp.concatenate([share, summed[:, 2 * pw :]], axis=1).astype(bf16)
        every = exchange(jnp.broadcast_to(share[None], (16,) + share.shape), ZY)
        same_b = swap(give_b, "xl")
        diff_b = lax.ppermute(give_b, ("xl", "xh"), both_flip)
        keep_c, cross_c, same_a_c, diff_a_c = (swap(v, "c") for v in (keep, cross, same_a, diff_a))
        every, keep_c, cross_c, same_a_c, diff_a_c, same_b, diff_b = tie(
            every, keep_c, cross_c, same_a_c, diff_a_c, same_b, diff_b
        )
        every, vec_give = tie(every, vec_give)
        every_c = swap(every, "c")
        coeffs_x = swap(every[:, :, : 2 * pw].reshape(quarter, 2 * pw), "xl")
        coeffs, mixed, update = expand(place, every, every_c, wide_high, wide_low, vecs, n_orbs)

    with jax.named_scope("transpose_out"):
        back = exchange(update, ZY)

    with jax.named_scope("density"):
        vec_keep_x = lax.ppermute(vec_give, ("xl", "xh"), both_flip)
        vec_keep_xc = swap(vec_keep_x, "c")
        same_b_c, diff_b_c = swap(same_b, "c"), swap(diff_b, "c")
        coeffs_y = swap(coeffs_x, "c")
        density = density_of(
            place,
            window,
            coeffs,
            [coeffs_x, coeffs_y],
            mixed,
            [weight_own, weight_oth],
            [vec_keep, vec_keep_c, vec_keep_x, vec_keep_xc],
            [
                ([keep], [same_a, same_b]),
                ([keep_c], [same_a_c, same_b_c]),
                ([cross], [diff_a, diff_b]),
                ([cross_c], [diff_a_c, diff_b_c]),
            ],
        )

    with jax.named_scope("subtract"):
        back, density = tie(back, density)
        out = subtract(eigvecs, back)
    return (out, density)


def cost(flops, bytes_accessed):
    return pl.CostEstimate(flops=flops, bytes_accessed=bytes_accessed, transcendentals=0)


def pack_kernel(side, orbs, panel_one, panel_two, extra, give, keep, *scratch):
    orbs_v, one_v, two_v, give_v, keep_v, sems = scratch
    parts, n_orbs, half = keep.shape
    n_vec = panel_one.shape[0]
    step = parts // STEPS
    loads = [
        pltpu.make_async_copy(panel_one, one_v, sems.at[0]),
        pltpu.make_async_copy(panel_two, two_v, sems.at[1]),
    ]
    for i in range(STEPS):
        at = pl.ds(i * step * 2 * half, step * 2 * half)
        loads.append(pltpu.make_async_copy(orbs.at[:, at], orbs_v.at[:, at], sems.at[2 + i]))
    for load in loads:
        load.start()
    for load in loads[:2]:
        load.wait()
    stores = []
    for i in range(STEPS):
        loads[2 + i].wait()
        for part in range(i * step, (i + 1) * step):
            for out, which in ((keep_v, side[0]), (give_v, 1 - side[0])):
                at = pl.multiple_of((2 * part + which) * half, half)
                out[part, :n_orbs, :] = orbs_v[:, pl.ds(at, half)].astype(jnp.bfloat16)
            for which in range(2):
                at = pl.ds((2 * part + which) * half, half)
                rows = pl.ds(n_orbs + which * 2 * n_vec, 2 * n_vec)
                both = jnp.concatenate([one_v[:, at], two_v[:, at]], axis=0)
                give_v[part, rows, :] = both
            give_v[part, pl.ds(n_orbs + 4 * n_vec, 16), :] = extra[...]
        at = pl.ds(i * step, step)
        for j, (source, target) in enumerate(((give_v, give), (keep_v, keep))):
            sem = sems.at[2 + (1 + j) * STEPS + i]
            stores.append(pltpu.make_async_copy(source.at[at], target.at[at], sem))
            stores[-1].start()
    for store in stores:
        store.wait()


def pack(side, orbs, panel_one, panel_two, extra, chunk):
    n_orbs, n_basis = orbs.shape
    parts, half = n_basis // chunk, chunk // 2
    n_give = n_orbs + 4 * panel_one.shape[0] + 16
    anywhere = pl.BlockSpec(memory_space=pl.ANY)
    give = (parts, n_give, half)
    keep = (parts, n_orbs, half)
    return pl.pallas_call(
        pack_kernel,
        out_shape=(
            jax.ShapeDtypeStruct(give, jnp.bfloat16),
            jax.ShapeDtypeStruct(keep, jnp.bfloat16),
        ),
        grid_spec=pltpu.PrefetchScalarGridSpec(
            num_scalar_prefetch=1,
            grid=(1,),
            in_specs=[anywhere, anywhere, anywhere]
            + [pl.BlockSpec(extra.shape, lambda i, _: (0, 0))],
            out_specs=(anywhere, anywhere),
            scratch_shapes=[
                pltpu.VMEM(orbs.shape, jnp.float32),
                pltpu.VMEM(panel_one.shape, jnp.bfloat16),
                pltpu.VMEM(panel_two.shape, jnp.bfloat16),
                pltpu.VMEM(give, jnp.bfloat16),
                pltpu.VMEM(keep, jnp.bfloat16),
                pltpu.SemaphoreType.DMA((2 + 3 * STEPS,)),
            ],
        ),
        compiler_params=pltpu.CompilerParams(vmem_limit_bytes=62 * 2**20),
        cost_estimate=cost(0, 7 * n_orbs * n_basis),
        name="pack",
    )(side, orbs, panel_one, panel_two, extra)


def subtract_kernel(orbs, update, out, orbs_v, update_v, sems):
    parts, _, chunk = update.shape
    step = parts // STEPS
    loads = []
    for i in range(STEPS):
        at, cols = pl.ds(i * step, step), pl.ds(i * step * chunk, step * chunk)
        loads.append(
            (
                pltpu.make_async_copy(update.at[at], update_v.at[at], sems.at[i]),
                pltpu.make_async_copy(orbs.at[:, cols], orbs_v.at[:, cols], sems.at[STEPS + i]),
            )
        )
        for load in loads[-1]:
            load.start()
    stores = []
    for i in range(STEPS):
        for load in loads[i]:
            load.wait()
        for part in range(i * step, (i + 1) * step):
            at = pl.ds(part * chunk, chunk)
            orbs_v[:, at] = orbs_v[:, at] - update_v[part].astype(jnp.float32)
        cols = pl.ds(i * step * chunk, step * chunk)
        sem = sems.at[2 * STEPS + i]
        stores.append(pltpu.make_async_copy(orbs_v.at[:, cols], out.at[:, cols], sem))
        stores[-1].start()
    for store in stores:
        store.wait()


def subtract(orbs, update):
    n_orbs, n_basis = orbs.shape
    anywhere = pl.BlockSpec(memory_space=pl.ANY)
    return pl.pallas_call(
        subtract_kernel,
        out_shape=jax.ShapeDtypeStruct(orbs.shape, jnp.float32),
        in_specs=[anywhere, anywhere],
        out_specs=anywhere,
        scratch_shapes=[
            pltpu.VMEM(orbs.shape, jnp.float32),
            pltpu.VMEM(update.shape, jnp.bfloat16),
            pltpu.SemaphoreType.DMA((3 * STEPS,)),
        ],
        compiler_params=pltpu.CompilerParams(vmem_limit_bytes=62 * 2**20),
        cost_estimate=cost(n_orbs * n_basis, 10 * n_orbs * n_basis),
        name="subtract_update",
    )(orbs, update)


def project_kernel(side, place, give, keep, vecs, vec_two, mine, theirs):
    blocks, n_own, lanes = mine.shape
    width = vecs.shape[1]
    proj = dot(give[...], vecs[1 - side[0]], ((1,), (1,)))
    proj = proj + dot(keep[...], vecs[side[0]], ((1,), (1,)))
    cross = dot(vecs[0], vec_two[0], ((1,), (1,)))
    cross = cross + dot(vecs[1], vec_two[1], ((1,), (1,)))

    def store(out):
        out[:, :, :width] = proj.astype(jnp.bfloat16).reshape(blocks, n_own, width)
        out[:, :, width:] = cross.astype(jnp.bfloat16).reshape(blocks, n_own, lanes - width)

    pl.when(pl.program_id(0) == place[1])(lambda: store(mine))
    pl.when(pl.program_id(0) != place[1])(lambda: store(theirs))


def project(side, place, give, keep, vecs, vec_two):
    n_orbs, half = give.shape
    width, n_two = vecs.shape[1], vec_two.shape[1]
    tile, lanes = n_orbs // 2, n_two // 2
    shape = (16, n_orbs // 32, width + lanes)
    return pl.pallas_call(
        project_kernel,
        out_shape=(jax.ShapeDtypeStruct(shape, jnp.bfloat16),) * 2,
        grid_spec=pltpu.PrefetchScalarGridSpec(
            num_scalar_prefetch=2,
            grid=(2,),
            in_specs=[
                pl.BlockSpec((tile, half), lambda i, *_: (i, 0)),
                pl.BlockSpec((tile, half), lambda i, *_: (i, 0)),
                pl.BlockSpec(vecs.shape, lambda i, *_: (0, 0, 0)),
                pl.BlockSpec((2, lanes, half), lambda i, *_: (0, i, 0)),
            ],
            out_specs=(pl.BlockSpec(shape, lambda i, *_: (0, 0, 0)),) * 2,
        ),
        compiler_params=pltpu.CompilerParams(vmem_limit_bytes=62 * 2**20),
        cost_estimate=cost(1, 1),
        name="project",
    )(side, place, give, keep, vecs, vec_two)


def expand_kernel(place, mine, theirs, wide_high, wide_low, vecs, coeffs, mixed, update):
    width, half = vecs.shape[1:]
    blocks, n_own, lanes = mine.shape
    lanes = lanes - width

    @pl.when(pl.program_id(0) == 0)
    def _():
        total = None
        for core, every in ((place[1], mine), (1 - place[1], theirs)):
            cross = every[:, :, width:].reshape(width, lanes)
            for wide in (wide_high, wide_low):
                term = dot(cross, wide[core], ((1,), (0,)))
                total = term if total is None else total + term
        row = lax.broadcasted_iota(jnp.int32, total.shape, 0)
        first = jnp.bitwise_and(lax.shift_right_logical(row, 3), 1) == 0
        mixed[...] = jnp.where(first, total, 0.0).astype(jnp.bfloat16)

    def fill(every):
        base = every[:, :, :width].reshape(blocks * n_own, width)
        fixed = base.astype(jnp.float32) - dot(base, mixed[...], ((1,), (0,)))
        fixed = fixed.astype(jnp.bfloat16)
        coeffs[...] = fixed
        for part in range(2):
            new = dot(fixed, vecs[part], ((1,), (0,))).astype(jnp.bfloat16)
            shape = update.shape[:2] + (half,)
            update[:, :, part * half : (part + 1) * half] = new.reshape(shape)

    pl.when(pl.program_id(0) == 0)(lambda: fill(mine))
    pl.when(pl.program_id(0) == 1)(lambda: fill(theirs))


def expand(place, mine, theirs, wide_high, wide_low, vecs, n_orbs):
    _, width, half = vecs.shape
    total = 2 * mine.shape[0] * mine.shape[1]
    wide_high, wide_low = (v.reshape(2, v.shape[0] // 2, width) for v in (wide_high, wide_low))

    def whole(value):
        return pl.BlockSpec(value.shape, lambda i, _: (0, 0, 0), pipeline_mode=pl.Buffered(1))

    def core(i, place):
        return i + place[1] - 2 * i * place[1]

    return pl.pallas_call(
        expand_kernel,
        out_shape=(
            jax.ShapeDtypeStruct((total, width), jnp.bfloat16),
            jax.ShapeDtypeStruct((width, width), jnp.bfloat16),
            jax.ShapeDtypeStruct((16, n_orbs, 2 * half), jnp.bfloat16),
        ),
        grid_spec=pltpu.PrefetchScalarGridSpec(
            num_scalar_prefetch=1,
            grid=(2,),
            in_specs=[whole(value) for value in (mine, theirs, wide_high, wide_low, vecs)],
            out_specs=(
                pl.BlockSpec((total // 2, width), lambda i, place: (core(i, place), 0)),
                pl.BlockSpec((width, width), lambda i, _: (0, 0)),
                pl.BlockSpec((8, n_orbs, 2 * half), lambda i, place: (core(i, place), 0, 0)),
            ),
        ),
        compiler_params=pltpu.CompilerParams(vmem_limit_bytes=62 * 2**20),
        cost_estimate=cost(2 * total * width * (width + 2 * half), 6 * 2**20),
        name="expand",
    )(place, mine, theirs, wide_high, wide_low, vecs)


def density_kernel(counts, place, win_orbs, win_vecs, *refs):
    coeffs, coeffs_x, coeffs_y, mixed, weight_own, weight_oth = refs[:6]
    vecs, refs = refs[6:10], refs[10:]
    n_pieces = sum(counts)
    pieces, refs = refs[:n_pieces], refs[n_pieces:]
    out, orbs_v, vecs_v, coeffs_v, raw_v, mixed_v, weight_v, sems = refs
    n_half, width = coeffs.shape
    n_orbs, tile = n_half // 16, win_orbs.shape[2]

    @pl.when(pl.program_id(0) == 0)
    def _():
        copies = []

        def fetch(source, target):
            copy = pltpu.make_async_copy(source, target, sems.at[len(copies)])
            copy.start()
            copies.append(copy)
            return copy

        factors = [fetch(coeffs, coeffs_v.at[0]), fetch(mixed, mixed_v)]
        factors += [fetch(coeffs_x, raw_v.at[0]), fetch(coeffs_y, raw_v.at[1])]
        factors += [fetch(weight_own, weight_v.at[0]), fetch(weight_oth, weight_v.at[1])]
        sides, used = [], 0
        for side in range(4):
            needed = [fetch(vecs[side], vecs_v.at[side])]
            for part in range(2):
                n = counts[2 * side + part]
                for i in range(n):
                    at = pl.ds(i * (n_half // n), n_half // n)
                    needed.append(fetch(pieces[used + i], orbs_v.at[2 * side + part, at]))
                used += n
            sides.append(needed)

        for copy in factors:
            copy.wait()
        for i, core in enumerate((place[1], 1 - place[1])):
            raw = raw_v[i]
            fixed = raw.astype(jnp.float32) - dot(raw, mixed_v[...], ((1,), (0,)))
            to = pl.multiple_of(core * (n_half // 2), n_half // 2)
            coeffs_v[1, pl.ds(to, n_half // 2), :] = fixed.astype(jnp.bfloat16)
        for side in range(4):
            for copy in sides[side]:
                copy.wait()
            for part in range(2):
                slot = 2 * side + part
                update = dot(coeffs_v[part], vecs_v[side], ((1,), (0,)))
                new = (orbs_v[slot].astype(jnp.float32) - update) * weight_v[part]
                orbs_v[slot] = new.astype(jnp.bfloat16)

    vec_tile = win_vecs[...].reshape(width, tile)
    turned = []
    for part in range(2):
        update = dot(coeffs_v[part], vec_tile, ((1,), (0,)))
        value = win_orbs[:, part * n_orbs : (part + 1) * n_orbs, :].reshape(n_half, tile)
        turned.append((value.astype(jnp.float32) - update).astype(jnp.bfloat16).T)
    for block in range(4):
        side = jnp.bitwise_xor(place[0], block)
        total = dot(turned[0], orbs_v[2 * side], ((1,), (0,)))
        out[:, block, :] = total + dot(turned[1], orbs_v[2 * side + 1], ((1,), (0,)))


def density_of(place, window, coeffs, others, mixed, weights, vecs, orbs):
    rows = window.shape[2]
    n_half, width = coeffs.shape
    half = vecs[0].shape[1]
    n_vec, n_orbs = width // 16, n_half // 16
    counts = [len(part) for side in orbs for part in side]
    pieces = [piece for side in orbs for part in side for piece in part]
    operands = [coeffs, *others, mixed, *weights, *vecs, *pieces]
    specs = [
        pl.BlockSpec((16, 2 * n_orbs, TILE), lambda i, _: (0, 0, i)),
        pl.BlockSpec((16, n_vec, TILE), lambda i, _: (0, 2 * n_orbs // n_vec, i)),
    ]
    return pl.pallas_call(
        functools.partial(density_kernel, counts),
        out_shape=jax.ShapeDtypeStruct((rows, 4, half), jnp.float32),
        grid_spec=pltpu.PrefetchScalarGridSpec(
            num_scalar_prefetch=1,
            grid=(rows // TILE,),
            in_specs=specs + [pl.BlockSpec(memory_space=pl.ANY)] * len(operands),
            out_specs=pl.BlockSpec((TILE, 4, half), lambda i, _: (i, 0, 0)),
            scratch_shapes=[
                pltpu.VMEM((8, n_half, half), jnp.bfloat16),
                pltpu.VMEM((4, width, half), jnp.bfloat16),
                pltpu.VMEM((2, n_half, width), jnp.bfloat16),
                pltpu.VMEM((2, n_half // 2, width), jnp.bfloat16),
                pltpu.VMEM((width, width), jnp.bfloat16),
                pltpu.VMEM((2, n_half, 1), jnp.float32),
                pltpu.SemaphoreType.DMA((len(operands),)),
            ],
        ),
        compiler_params=pltpu.CompilerParams(vmem_limit_bytes=62 * 2**20),
        cost_estimate=cost(16 * rows * n_half * half + 16 * n_half * width * half, 28 * 2**20),
        name="density",
    )(place, window, window, *operands)


def solution(mesh):
    mesh = Mesh(mesh.devices.reshape(4, 4, 2, 2, 2), ("z", "y", "xl", "xh", "c"))
    slab, grid = ("z", "y", "xl"), ("xh", "c")
    both = P(slab, grid)
    in_specs = (both, both, both, P(), P(), P(slab), P(), P())
    out_specs = (both, P(grid, None, slab))
    return jax.shard_map(body, mesh=mesh, in_specs=in_specs, out_specs=out_specs, check_vma=False)
```

```python
import functools
import math

import jax
import jax.numpy as jnp
from jax import lax
from jax.experimental import pallas as pl
from jax.experimental.pallas import tpu as pltpu
from jax.sharding import Mesh
from jax.sharding import PartitionSpec as P

OCC = 2048
R = 4096
ZY = ("z", "y")
ZYC = ("z", "y", "c")
TILE = 256
STEPS = 8


def dot(left, right, dims, **kwargs):
    return lax.dot_general(
        left, right, (dims, ((), ())), preferred_element_type=jnp.float32, **kwargs
    )


def swap(values, axis):
    return lax.ppermute(values, axis, [(0, 1), (1, 0)])


def exchange(values, axes):
    return lax.all_to_all(values, axes, 0, 0, tiled=True)


def tie(*values):
    return lax.optimization_barrier(values)


def pick(first, second, flag):
    return jnp.where(flag == 0, first, second)


def body(
    eigvecs, panel_one, panel_two, factor_one, factor_two, occupations, occupied_count, row_offset
):
    bf16 = jnp.bfloat16
    xl, xh, c = (lax.axis_index(name) for name in ("xl", "xh", "c"))
    zy = lax.axis_index(ZY)
    n_orbs, n_basis = eigvecs.shape
    n_vec = panel_one.shape[0]
    chunk = n_basis // 16
    half = chunk // 2
    pw = factor_one.shape[0]
    rows = R // 4

    n_all = 2 * n_vec
    side_xl = xl.astype(jnp.int32).reshape(1)
    place = jnp.stack([xh * 2 + c, c]).astype(jnp.int32)

    with jax.named_scope("pack"):
        occ_high = occupations.astype(bf16)
        rest = occupations - occ_high.astype(jnp.float32)
        occ_mid = rest.astype(bf16)
        occ_low = (rest - occ_mid.astype(jnp.float32)).astype(bf16)
        extra = jnp.zeros((16, half), bf16)
        extra = extra.at[:3, :n_orbs].set(jnp.stack([occ_high, occ_mid, occ_low]))
        give_p = pack(1 - side_xl, eigvecs, chunk, (panel_one, panel_two))

    with jax.named_scope("transpose_give"):
        got = exchange(give_p, ZY)

    with jax.named_scope("window_exchange"):
        start = row_offset[0] - (xh * 2 + c) * n_basis
        held, _ = tie(eigvecs, give_p)

        def cut(part):
            first = start + part * rows
            at = jnp.clip(first, 0, n_basis - rows)
            pieces = (held, panel_one, panel_two)
            pieces = [lax.dynamic_slice_in_dim(v, at, rows, 1).astype(bf16) for v in pieces]
            piece = jnp.concatenate(pieces)
            zeros = jnp.zeros_like(piece)
            piece = jnp.concatenate([zeros, piece, zeros], axis=1)
            shift = jnp.clip(first - at, -rows, rows)
            return lax.dynamic_slice_in_dim(piece, rows + shift, rows, 1)

        both_flip = [(i, 3 - i) for i in range(4)]
        from_xh = swap(cut((1 - xh) * 2 + c), "xh")
        from_both = lax.ppermute(cut((1 - xh) * 2 + 1 - c), ("xh", "c"), both_flip)
        from_c = swap(cut(xh * 2 + 1 - c), "c")
        mine = (cut(xh * 2 + c) + from_c) + (from_xh + from_both)
        mine_x = swap(mine, "xl")

        def by_xl(own, other, axis):
            return jnp.stack([pick(own, other, xl), pick(other, own, xl)], axis=axis)

        win_vecs = by_xl(mine[n_orbs:], mine_x[n_orbs:], 0).reshape(2 * n_all, rows)
        window = jnp.concatenate([mine[:n_orbs], mine_x[:n_orbs], win_vecs], axis=0)
        keep_p = pack(side_xl, eigvecs, chunk, (extra,))
        got, keep_p, window = tie(got, keep_p, window)
        window = lax.all_gather(window, ZY, axis=0)

    with jax.named_scope("transpose_keep"):
        kept = exchange(keep_p, ZY)
        give = got[:, :n_orbs].reshape(16 * n_orbs, half)
        vec_own = [got[:, n_orbs + i * n_all : n_orbs + (i + 1) * n_all] for i in range(2)]
        vec_oth = [swap(value, "xl") for value in vec_own]
        quarter = 8 * n_orbs
        diff_oth = lax.ppermute(give, ("xl", "xh"), both_flip)
        factor_one, factor_two, give, *vec_oth = tie(factor_one, factor_two, give, *vec_oth)
        give_a, give_b = give[:quarter], give[quarter:]
        same_a = swap(give_a, "xl")

        vecs = jnp.stack([by_xl(own, oth, 1) for own, oth in zip(vec_own, vec_oth)])
        vec_two = vecs.reshape(2, 32, 2, n_vec, half)[:, :, 1].reshape(2, pw, half)
        vecs = vecs.reshape(2, 2 * pw, half)
        vec_keep = lax.dynamic_index_in_dim(vecs, xl, 0, keepdims=False)
        vec_give = lax.dynamic_index_in_dim(vecs, 1 - xl, 0, keepdims=False)

        high = lax.Precision.HIGHEST
        at_v = jnp.arange(pw, dtype=jnp.int32)[:, None]
        at_q = jnp.arange(2 * pw, dtype=jnp.int32)[None]
        factor = jnp.zeros((2 * pw, 2 * pw), jnp.float32)
        for panel, one in enumerate((factor_one, factor_two)):
            spot = (at_v // n_vec) * 2 * n_vec + panel * n_vec + at_v % n_vec
            place_of = (at_q == spot).astype(jnp.float32)
            wide = dot(one, place_of, ((0,), (0,)), precision=high)
            factor = factor + dot(place_of, wide, ((0,), (0,)), precision=high)
        wide_high = wide.astype(bf16)
        wide_low = (wide - wide_high.astype(jnp.float32)).astype(bf16)
        vec_keep_c = swap(vec_keep, "c")
        kept, same_a, diff_oth, vecs, vec_two, vec_keep = tie(
            kept, same_a, diff_oth, vecs, vec_two, vec_keep
        )
        kept, vec_keep_c = tie(kept, vec_keep_c)
        kept, factor, wide_high, wide_low = tie(kept, factor, wide_high, wide_low)
        keep = kept[:, :n_orbs].reshape(16 * n_orbs, half)
        occ_own = kept[:, n_orbs:, :128]

    with jax.named_scope("project"):
        cross = swap(keep, "xh")
        occ_oth = swap(occ_own, "xl")
        parts, parts_c = project(side_xl, place, give, kept, vecs, vec_two)
        parts = parts.astype(jnp.float32) + swap(parts_c, "c").astype(jnp.float32)
        summed = exchange(parts.astype(bf16), ZY)
        summed, cross, occ_oth = tie(summed, cross, occ_oth)
        summed = summed.astype(jnp.float32).sum(0)
        summed = summed + swap(summed, "xh")
        summed, give_b, vec_give = tie(summed, give_b, vec_give)

    with jax.named_scope("coefficients"):
        share = dot(summed[:, : 2 * pw], factor, ((1,), (0,)), precision=high)
        share = jnp.concatenate([share, summed[:, 2 * pw :]], axis=1).astype(bf16)
        every = exchange(jnp.broadcast_to(share[None], (16,) + share.shape), ZY)
        def weight_of(occ, side):
            occ = occ[:, :3, :n_orbs].astype(jnp.float32)
            occ = (occ[:, 0] + occ[:, 1]) + occ[:, 2]
            index = (jnp.arange(16, dtype=jnp.int32)[:, None] * 2 + side) * n_orbs
            index = index + jnp.arange(n_orbs, dtype=jnp.int32)[None]
            occ = jnp.where(index < occupied_count[0], occ / math.sqrt(OCC), jnp.float32(0.0))
            return occ.reshape(16 * n_orbs, 1)

        weight_own, weight_oth = weight_of(occ_own, xl), weight_of(occ_oth, 1 - xl)
        same_b = swap(give_b, "xl")
        vec_keep_x = lax.ppermute(vec_give, ("xl", "xh"), both_flip)
        keep_c, cross_c, same_a_c, diff_c = (swap(v, "c") for v in (keep, cross, same_a, diff_oth))
        every, keep_c, cross_c, same_a_c, diff_c, same_b, vec_keep_x = tie(
            every, keep_c, cross_c, same_a_c, diff_c, same_b, vec_keep_x
        )
        every, weight_own, weight_oth = tie(every, weight_own, weight_oth)
        every_c = swap(every, "c")
        coeffs_x = swap(every[:, :, : 2 * pw].reshape(quarter, 2 * pw), "xl")
        coeffs, mixed, update = expand(place, every, every_c, wide_high, wide_low, vecs, n_orbs)

    with jax.named_scope("transpose_out"):
        back = exchange(update, ZY)

    with jax.named_scope("density"):
        vec_keep_xc, same_b_c = swap(vec_keep_x, "c"), swap(same_b, "c")
        coeffs_y = swap(coeffs_x, "c")
        density = density_of(
            place,
            window,
            coeffs,
            [coeffs_x, coeffs_y],
            mixed,
            [weight_own, weight_oth],
            [vec_keep, vec_keep_c, vec_keep_x, vec_keep_xc],
            [
                ([keep], [same_a, same_b]),
                ([keep_c], [same_a_c, same_b_c]),
                ([cross], [diff_oth]),
                ([cross_c], [diff_c]),
            ],
        )

    with jax.named_scope("subtract"):
        back, density = tie(back, density)
        out = subtract(eigvecs, back)
    return (out, density)


def cost(flops, bytes_accessed):
    return pl.CostEstimate(flops=flops, bytes_accessed=bytes_accessed, transcendentals=0)


def pack_kernel(n_tails, which, orbs, *refs):
    tails, out, orbs_v, out_v = refs[:n_tails], refs[n_tails], refs[n_tails + 1], refs[n_tails + 2]
    sems, tails_v = refs[-1], refs[n_tails + 3 : -1]
    parts, n_orbs, half = orbs_v.shape
    loads = []
    for i in range(parts):
        at = pl.ds(pl.multiple_of((2 * i + which[0]) * half, half), half)
        loads.append(pltpu.make_async_copy(orbs.at[:, at], orbs_v.at[i], sems.at[i]))
    for i, (tail, tail_v) in enumerate(zip(tails, tails_v)):
        loads.append(pltpu.make_async_copy(tail, tail_v, sems.at[parts + i]))
    for load in loads:
        load.start()
    for load in loads[parts:]:
        load.wait()
    stores = []
    for i in range(parts):
        loads[i].wait()
        out_v[i, :n_orbs, :] = orbs_v[i].astype(jnp.bfloat16)
        if n_tails == 2:
            for side in range(2):
                at = pl.ds((2 * i + side) * half, half)
                both = jnp.concatenate([tail_v[:, at] for tail_v in tails_v], axis=0)
                out_v[i, pl.ds(n_orbs + side * 16, 16), :] = both
        else:
            out_v[i, pl.ds(n_orbs, 16), :] = tails_v[0][...]
        if i % 4 == 3:
            at = pl.ds(i - 3, 4)
            sem = sems.at[parts + n_tails + i // 4]
            stores.append(pltpu.make_async_copy(out_v.at[at], out.at[at], sem))
            stores[-1].start()
    for store in stores:
        store.wait()


def pack(which, orbs, chunk, tails):
    n_orbs, n_basis = orbs.shape
    parts, half = n_basis // chunk, chunk // 2
    anywhere = pl.BlockSpec(memory_space=pl.ANY)
    shape = (parts, n_orbs + 16 * (2 if len(tails) == 2 else 1), half)
    return pl.pallas_call(
        functools.partial(pack_kernel, len(tails)),
        out_shape=jax.ShapeDtypeStruct(shape, jnp.bfloat16),
        in_specs=[pl.BlockSpec(memory_space=pltpu.SMEM)] + [anywhere] * (1 + len(tails)),
        out_specs=anywhere,
        scratch_shapes=[
            pltpu.VMEM((parts, n_orbs, half), jnp.float32),
            pltpu.VMEM(shape, jnp.bfloat16),
            *[pltpu.VMEM(tail.shape, jnp.bfloat16) for tail in tails],
            pltpu.SemaphoreType.DMA((parts + len(tails) + parts // 4,)),
        ],
        compiler_params=pltpu.CompilerParams(vmem_limit_bytes=62 * 2**20),
        cost_estimate=cost(0, 3 * n_orbs * n_basis),
        name="pack_vectors" if len(tails) == 2 else "pack_weights",
    )(which, orbs, *tails)


def subtract_kernel(orbs, update, out, orbs_v, update_v, sems):
    parts, _, chunk = update.shape
    step = parts // STEPS
    loads = []
    for i in range(STEPS):
        at, cols = pl.ds(i * step, step), pl.ds(i * step * chunk, step * chunk)
        loads.append(
            (
                pltpu.make_async_copy(update.at[at], update_v.at[at], sems.at[i]),
                pltpu.make_async_copy(orbs.at[:, cols], orbs_v.at[:, cols], sems.at[STEPS + i]),
            )
        )
        for load in loads[-1]:
            load.start()
    stores = []
    for i in range(STEPS):
        for load in loads[i]:
            load.wait()
        for part in range(i * step, (i + 1) * step):
            at = pl.ds(part * chunk, chunk)
            orbs_v[:, at] = orbs_v[:, at] - update_v[part].astype(jnp.float32)
        cols = pl.ds(i * step * chunk, step * chunk)
        sem = sems.at[2 * STEPS + i]
        stores.append(pltpu.make_async_copy(orbs_v.at[:, cols], out.at[:, cols], sem))
        stores[-1].start()
    for store in stores:
        store.wait()


def subtract(orbs, update):
    n_orbs, n_basis = orbs.shape
    anywhere = pl.BlockSpec(memory_space=pl.ANY)
    return pl.pallas_call(
        subtract_kernel,
        out_shape=jax.ShapeDtypeStruct(orbs.shape, jnp.float32),
        in_specs=[anywhere, anywhere],
        out_specs=anywhere,
        scratch_shapes=[
            pltpu.VMEM(orbs.shape, jnp.float32),
            pltpu.VMEM(update.shape, jnp.bfloat16),
            pltpu.SemaphoreType.DMA((3 * STEPS,)),
        ],
        compiler_params=pltpu.CompilerParams(vmem_limit_bytes=62 * 2**20),
        cost_estimate=cost(n_orbs * n_basis, 10 * n_orbs * n_basis),
        name="subtract_update",
    )(orbs, update)


def project_kernel(side, place, give, keep, vecs, vec_two, mine, theirs, blocks_v, sems):
    blocks, n_own, lanes = mine.shape
    width = vecs.shape[1]
    n_rows, n_two = blocks * n_own, lanes - width
    stores = []
    for i, (out, half) in enumerate(((theirs, 1 - place[1]), (mine, place[1]))):
        at = pl.ds(pl.multiple_of(half * n_rows, n_rows), n_rows)
        proj = dot(give[at, :], vecs[1 - side[0]], ((1,), (1,)))
        rows = keep[pl.ds(half * (blocks // 2), blocks // 2), : 2 * n_own, :]
        rows = rows.reshape(n_rows, keep.shape[2])
        proj = proj + dot(rows, vecs[side[0]], ((1,), (1,)))
        blocks_v[i, :, :, :width] = proj.astype(jnp.bfloat16).reshape(blocks, n_own, width)
        at = pl.ds(pl.multiple_of(half * n_two, n_two), n_two)
        cross = dot(vecs[0], vec_two[0, at, :], ((1,), (1,)))
        cross = cross + dot(vecs[1], vec_two[1, at, :], ((1,), (1,)))
        blocks_v[i, :, :, width:] = cross.astype(jnp.bfloat16).reshape(blocks, n_own, n_two)
        stores.append(pltpu.make_async_copy(blocks_v.at[i], out, sems.at[i]))
        stores[-1].start()
    for store in stores:
        store.wait()


def specs_of(n_scalars, n_arrays):
    scalar = pl.BlockSpec(memory_space=pltpu.SMEM)
    return [scalar] * n_scalars + [pl.BlockSpec(memory_space=pltpu.VMEM)] * n_arrays


def project(side, place, give, keep, vecs, vec_two):
    shape = (16, give.shape[0] // 32, vecs.shape[1] + vec_two.shape[1] // 2)
    return pl.pallas_call(
        project_kernel,
        out_shape=(jax.ShapeDtypeStruct(shape, jnp.bfloat16),) * 2,
        in_specs=specs_of(2, 4),
        out_specs=(pl.BlockSpec(memory_space=pltpu.HBM),) * 2,
        scratch_shapes=[
            pltpu.VMEM((2,) + shape, jnp.bfloat16),
            pltpu.SemaphoreType.DMA((2,)),
        ],
        compiler_params=pltpu.CompilerParams(vmem_limit_bytes=20 * 2**20),
        cost_estimate=cost(1, 1),
        name="project",
    )(side, place, give, keep, vecs, vec_two)


def expand_kernel(place, mine, theirs, wide_high, wide_low, vecs, *rest):
    coeffs, mixed, update, coeffs_v, mixed_v, update_v, sems = rest
    width, half = vecs.shape[1:]
    blocks, n_own, lanes = mine.shape
    lanes = lanes - width
    n_rows, n_parts, n_orbs = blocks * n_own, update.shape[0] // 2, update.shape[1]
    halves = ((place[1], mine), (1 - place[1], theirs))
    total = None
    for core, every in halves:
        cross = every[:, :, width:].reshape(width, lanes)
        for wide in (wide_high, wide_low):
            term = dot(cross, wide[core], ((1,), (0,)))
            total = term if total is None else total + term
    row = lax.broadcasted_iota(jnp.int32, total.shape, 0)
    first = jnp.bitwise_and(lax.shift_right_logical(row, 3), 1) == 0
    mixed_v[...] = jnp.where(first, total, 0.0).astype(jnp.bfloat16)
    stores = [pltpu.make_async_copy(mixed_v, mixed, sems.at[0])]
    stores[0].start()
    for i, (core, every) in enumerate(halves):
        base = every[:, :, :width].reshape(n_rows, width)
        fixed = base.astype(jnp.float32) - dot(base, mixed_v[...], ((1,), (0,)))
        fixed = fixed.astype(jnp.bfloat16)
        coeffs_v[i] = fixed
        for part in range(2):
            new = dot(fixed, vecs[part], ((1,), (0,))).astype(jnp.bfloat16)
            new = new.reshape(n_parts, n_orbs, half)
            update_v[i, :, :, part * half : (part + 1) * half] = new
        at = pl.ds(pl.multiple_of(core * n_rows, n_rows), n_rows)
        stores.append(pltpu.make_async_copy(coeffs_v.at[i], coeffs.at[at], sems.at[1 + i]))
        at = pl.ds(core * n_parts, n_parts)
        stores.append(pltpu.make_async_copy(update_v.at[i], update.at[at], sems.at[3 + i]))
        for store in stores[-2:]:
            store.start()
    for store in stores:
        store.wait()


def expand(place, mine, theirs, wide_high, wide_low, vecs, n_orbs):
    _, width, half = vecs.shape
    total = 2 * mine.shape[0] * mine.shape[1]
    wide_high, wide_low = (v.reshape(2, v.shape[0] // 2, width) for v in (wide_high, wide_low))
    return pl.pallas_call(
        expand_kernel,
        out_shape=(
            jax.ShapeDtypeStruct((total, width), jnp.bfloat16),
            jax.ShapeDtypeStruct((width, width), jnp.bfloat16),
            jax.ShapeDtypeStruct((16, n_orbs, 2 * half), jnp.bfloat16),
        ),
        in_specs=specs_of(1, 5),
        out_specs=(pl.BlockSpec(memory_space=pltpu.HBM),) * 3,
        scratch_shapes=[
            pltpu.VMEM((2, total // 2, width), jnp.bfloat16),
            pltpu.VMEM((width, width), jnp.bfloat16),
            pltpu.VMEM((2, 8, n_orbs, 2 * half), jnp.bfloat16),
            pltpu.SemaphoreType.DMA((5,)),
        ],
        compiler_params=pltpu.CompilerParams(vmem_limit_bytes=60 * 2**20 + 768 * 2**10),
        cost_estimate=cost(2 * total * width * (width + 2 * half), 6 * 2**20),
        name="expand",
    )(place, mine, theirs, wide_high, wide_low, vecs)


def density_kernel(counts, place, win_orbs, win_vecs, *refs):
    coeffs, coeffs_x, coeffs_y, mixed, weight_own, weight_oth = refs[:6]
    vecs, refs = refs[6:10], refs[10:]
    n_pieces = sum(counts)
    pieces, refs = refs[:n_pieces], refs[n_pieces:]
    out, orbs_v, vecs_v, coeffs_v, raw_v, mixed_v, weight_v, sems = refs
    n_half, width = coeffs.shape
    n_orbs, tile = n_half // 16, win_orbs.shape[2]

    @pl.when(pl.program_id(0) == 0)
    def _():
        copies = []

        def fetch(source, target):
            copy = pltpu.make_async_copy(source, target, sems.at[len(copies)])
            copy.start()
            copies.append(copy)
            return copy

        factors = [fetch(coeffs, coeffs_v.at[0]), fetch(mixed, mixed_v)]
        factors += [fetch(coeffs_x, raw_v.at[0]), fetch(coeffs_y, raw_v.at[1])]
        factors += [fetch(weight_own, weight_v.at[0]), fetch(weight_oth, weight_v.at[1])]
        sides, used = [], 0
        for side in range(4):
            needed = [fetch(vecs[side], vecs_v.at[side])]
            for part in range(2):
                n = counts[2 * side + part]
                for i in range(n):
                    at = pl.ds(i * (n_half // n), n_half // n)
                    needed.append(fetch(pieces[used + i], orbs_v.at[2 * side + part, at]))
                used += n
            sides.append(needed)

        for copy in factors:
            copy.wait()
        for i, core in enumerate((place[1], 1 - place[1])):
            raw = raw_v[i]
            fixed = raw.astype(jnp.float32) - dot(raw, mixed_v[...], ((1,), (0,)))
            to = pl.multiple_of(core * (n_half // 2), n_half // 2)
            coeffs_v[1, pl.ds(to, n_half // 2), :] = fixed.astype(jnp.bfloat16)
        for side in range(4):
            for copy in sides[side]:
                copy.wait()
            for part in range(2):
                slot = 2 * side + part
                update = dot(coeffs_v[part], vecs_v[side], ((1,), (0,)))
                new = (orbs_v[slot].astype(jnp.float32) - update) * weight_v[part]
                orbs_v[slot] = new.astype(jnp.bfloat16)

    vec_tile = win_vecs[...].reshape(width, tile)
    turned = []
    for part in range(2):
        update = dot(coeffs_v[part], vec_tile, ((1,), (0,)))
        value = win_orbs[:, part * n_orbs : (part + 1) * n_orbs, :].reshape(n_half, tile)
        turned.append((value.astype(jnp.float32) - update).astype(jnp.bfloat16).T)
    for block in range(4):
        side = jnp.bitwise_xor(place[0], block)
        total = dot(turned[0], orbs_v[2 * side], ((1,), (0,)))
        out[:, block, :] = total + dot(turned[1], orbs_v[2 * side + 1], ((1,), (0,)))


def density_of(place, window, coeffs, others, mixed, weights, vecs, orbs):
    rows = window.shape[2]
    n_half, width = coeffs.shape
    half = vecs[0].shape[1]
    n_vec, n_orbs = width // 16, n_half // 16
    counts = [len(part) for side in orbs for part in side]
    pieces = [piece for side in orbs for part in side for piece in part]
    operands = [coeffs, *others, mixed, *weights, *vecs, *pieces]
    specs = [
        pl.BlockSpec((16, 2 * n_orbs, TILE), lambda i, _: (0, 0, i)),
        pl.BlockSpec((16, n_vec, TILE), lambda i, _: (0, 2 * n_orbs // n_vec, i)),
    ]
    return pl.pallas_call(
        functools.partial(density_kernel, counts),
        out_shape=jax.ShapeDtypeStruct((rows, 4, half), jnp.float32),
        grid_spec=pltpu.PrefetchScalarGridSpec(
            num_scalar_prefetch=1,
            grid=(rows // TILE,),
            in_specs=specs + [pl.BlockSpec(memory_space=pl.ANY)] * len(operands),
            out_specs=pl.BlockSpec((TILE, 4, half), lambda i, _: (i, 0, 0)),
            scratch_shapes=[
                pltpu.VMEM((8, n_half, half), jnp.bfloat16),
                pltpu.VMEM((4, width, half), jnp.bfloat16),
                pltpu.VMEM((2, n_half, width), jnp.bfloat16),
                pltpu.VMEM((2, n_half // 2, width), jnp.bfloat16),
                pltpu.VMEM((width, width), jnp.bfloat16),
                pltpu.VMEM((2, n_half, 1), jnp.float32),
                pltpu.SemaphoreType.DMA((len(operands),)),
            ],
        ),
        compiler_params=pltpu.CompilerParams(vmem_limit_bytes=62 * 2**20),
        cost_estimate=cost(16 * rows * n_half * half + 16 * n_half * width * half, 28 * 2**20),
        name="density",
    )(place, window, window, *operands)


def solution(mesh):
    mesh = Mesh(mesh.devices.reshape(4, 4, 2, 2, 2), ("z", "y", "xl", "xh", "c"))
    slab, grid = ("z", "y", "xl"), ("xh", "c")
    both = P(slab, grid)
    in_specs = (both, both, both, P(), P(), P(slab), P(), P())
    out_specs = (both, P(grid, None, slab))
    return jax.shard_map(body, mesh=mesh, in_specs=in_specs, out_specs=out_specs, check_vma=False)
```

```python
import functools
import math

import jax
import jax.numpy as jnp
from jax import lax
from jax.experimental import pallas as pl
from jax.experimental.pallas import tpu as pltpu
from jax.sharding import Mesh
from jax.sharding import PartitionSpec as P

OCC = 2048
R = 4096
ZY = ("z", "y")
ZYC = ("z", "y", "c")
TILE = 256
STEPS = 8


def dot(left, right, dims, **kwargs):
    return lax.dot_general(
        left, right, (dims, ((), ())), preferred_element_type=jnp.float32, **kwargs
    )


def swap(values, axis):
    return lax.ppermute(values, axis, [(0, 1), (1, 0)])


def exchange(values, axes):
    return lax.all_to_all(values, axes, 0, 0, tiled=True)


def tie(*values):
    return lax.optimization_barrier(values)


def pick(first, second, flag):
    return jnp.where(flag == 0, first, second)


def body(
    eigvecs, panel_one, panel_two, factor_one, factor_two, occupations, occupied_count, row_offset
):
    bf16 = jnp.bfloat16
    xl, xh, c = (lax.axis_index(name) for name in ("xl", "xh", "c"))
    zy = lax.axis_index(ZY)
    n_orbs, n_basis = eigvecs.shape
    n_vec = panel_one.shape[0]
    chunk = n_basis // 16
    half = chunk // 2
    pw = factor_one.shape[0]
    rows = R // 4

    n_all = 2 * n_vec
    side_xl = xl.astype(jnp.int32).reshape(1)
    place = jnp.stack([xh * 2 + c, c]).astype(jnp.int32)

    with jax.named_scope("pack"):
        occ_high = occupations.astype(bf16)
        rest = occupations - occ_high.astype(jnp.float32)
        occ_mid = rest.astype(bf16)
        occ_low = (rest - occ_mid.astype(jnp.float32)).astype(bf16)
        extra = jnp.zeros((16, half), bf16)
        extra = extra.at[:3, :n_orbs].set(jnp.stack([occ_high, occ_mid, occ_low]))
        give_p = pack(1 - side_xl, eigvecs, chunk, (panel_one, panel_two))

    with jax.named_scope("transpose_give"):
        got = exchange(give_p, ZY)

    with jax.named_scope("window_exchange"):
        start = row_offset[0] - (xh * 2 + c) * n_basis
        held, _ = tie(eigvecs, give_p)

        def cut(part):
            first = start + part * rows
            at = jnp.clip(first, 0, n_basis - rows)
            pieces = (held, panel_one, panel_two)
            pieces = [lax.dynamic_slice_in_dim(v, at, rows, 1).astype(bf16) for v in pieces]
            piece = jnp.concatenate(pieces)
            zeros = jnp.zeros_like(piece)
            piece = jnp.concatenate([zeros, piece, zeros], axis=1)
            shift = jnp.clip(first - at, -rows, rows)
            return lax.dynamic_slice_in_dim(piece, rows + shift, rows, 1)

        both_flip = [(i, 3 - i) for i in range(4)]
        from_xh = swap(cut((1 - xh) * 2 + c), "xh")
        from_both = lax.ppermute(cut((1 - xh) * 2 + 1 - c), ("xh", "c"), both_flip)
        from_c = swap(cut(xh * 2 + 1 - c), "c")
        mine = (cut(xh * 2 + c) + from_c) + (from_xh + from_both)
        mine_x = swap(mine, "xl")

        def by_xl(own, other, axis):
            return jnp.stack([pick(own, other, xl), pick(other, own, xl)], axis=axis)

        win_vecs = by_xl(mine[n_orbs:], mine_x[n_orbs:], 0).reshape(2 * n_all, rows)
        window = jnp.concatenate([mine[:n_orbs], mine_x[:n_orbs], win_vecs], axis=0)
        keep_p = pack(side_xl, eigvecs, chunk, (extra,))
        got, keep_p, window = tie(got, keep_p, window)

    with jax.named_scope("transpose_keep"):
        kept = exchange(keep_p, ZY)
        give = got[:, :n_orbs].reshape(16 * n_orbs, half)
        vec_own = [got[:, n_orbs + i * n_all : n_orbs + (i + 1) * n_all] for i in range(2)]
        vec_oth = [swap(value, "xl") for value in vec_own]
        quarter = 8 * n_orbs
        diff_a = lax.ppermute(give[:quarter], ("xl", "xh"), both_flip)
        diff_b = lax.ppermute(give[quarter:], ("xl", "xh"), both_flip)
        factor_one, factor_two, give, diff_a, *vec_oth = tie(
            factor_one, factor_two, give, diff_a, *vec_oth
        )
        give_a, give_b = give[:quarter], give[quarter:]
        same_a = swap(give_a, "xl")

        vecs = jnp.stack([by_xl(own, oth, 1) for own, oth in zip(vec_own, vec_oth)])
        vec_two = vecs.reshape(2, 32, 2, n_vec, half)[:, :, 1].reshape(2, pw, half)
        vecs = vecs.reshape(2, 2 * pw, half)
        vec_keep = lax.dynamic_index_in_dim(vecs, xl, 0, keepdims=False)
        vec_give = lax.dynamic_index_in_dim(vecs, 1 - xl, 0, keepdims=False)

        high = lax.Precision.HIGHEST
        at_v = jnp.arange(pw, dtype=jnp.int32)[:, None]
        at_q = jnp.arange(2 * pw, dtype=jnp.int32)[None]
        factor = jnp.zeros((2 * pw, 2 * pw), jnp.float32)
        for panel, one in enumerate((factor_one, factor_two)):
            spot = (at_v // n_vec) * 2 * n_vec + panel * n_vec + at_v % n_vec
            place_of = (at_q == spot).astype(jnp.float32)
            wide = dot(one, place_of, ((0,), (0,)), precision=high)
            factor = factor + dot(place_of, wide, ((0,), (0,)), precision=high)
        wide_high = wide.astype(bf16)
        wide_low = (wide - wide_high.astype(jnp.float32)).astype(bf16)
        vec_keep_c = swap(vec_keep, "c")
        kept, same_a, diff_b, vecs, vec_two, vec_keep, vec_keep_c, *ready = tie(
            kept, same_a, diff_b, vecs, vec_two, vec_keep, vec_keep_c, window, factor, wide_high,
            wide_low,
        )
        window, factor, wide_high, wide_low = ready
        window = lax.all_gather(window, ZY, axis=0)
        occ_own = kept[:, n_orbs:, :128]

    with jax.named_scope("project"):
        occ_oth = swap(occ_own, "xl")
        parts, parts_c, keep = project(side_xl, place, give, kept, vecs, vec_two)
        keep = keep.reshape(16 * n_orbs, half)
        cross = swap(keep, "xh")
        parts = parts.astype(jnp.float32) + swap(parts_c, "c").astype(jnp.float32)
        summed = exchange(parts.astype(bf16), ZY)
        summed, cross, occ_oth = tie(summed, cross, occ_oth)
        summed = summed.astype(jnp.float32).sum(0)
        summed = summed + swap(summed, "xh")
        summed, give_b, vec_give = tie(summed, give_b, vec_give)

    with jax.named_scope("coefficients"):
        share = dot(summed[:, : 2 * pw], factor, ((1,), (0,)), precision=high)
        share = jnp.concatenate([share, summed[:, 2 * pw :]], axis=1).astype(bf16)
        every = exchange(jnp.broadcast_to(share[None], (16,) + share.shape), ZY)
        def weight_of(occ, side):
            occ = occ[:, :3, :n_orbs].astype(jnp.float32)
            occ = (occ[:, 0] + occ[:, 1]) + occ[:, 2]
            index = (jnp.arange(16, dtype=jnp.int32)[:, None] * 2 + side) * n_orbs
            index = index + jnp.arange(n_orbs, dtype=jnp.int32)[None]
            occ = jnp.where(index < occupied_count[0], occ / math.sqrt(OCC), jnp.float32(0.0))
            return occ.reshape(16 * n_orbs, 1)

        weight_own, weight_oth = weight_of(occ_own, xl), weight_of(occ_oth, 1 - xl)
        same_b = swap(give_b, "xl")
        vec_keep_x = lax.ppermute(vec_give, ("xl", "xh"), both_flip)
        keep_c, cross_c, same_a_c, diff_a_c, diff_b_c = (
            swap(v, "c") for v in (keep, cross, same_a, diff_a, diff_b)
        )
        every, keep_c, cross_c, same_a_c, diff_a_c, diff_b_c, same_b, vec_keep_x = tie(
            every, keep_c, cross_c, same_a_c, diff_a_c, diff_b_c, same_b, vec_keep_x
        )
        every, weight_own, weight_oth = tie(every, weight_own, weight_oth)
        every_c = swap(every, "c")
        coeffs_x = swap(every[:, :, : 2 * pw].reshape(quarter, 2 * pw), "xl")
        coeffs, mixed, update = expand(place, every, every_c, wide_high, wide_low, vecs, n_orbs)

    with jax.named_scope("transpose_out"):
        back = exchange(update, ZY)

    with jax.named_scope("density"):
        vec_keep_xc, same_b_c = swap(vec_keep_x, "c"), swap(same_b, "c")
        coeffs_y = swap(coeffs_x, "c")
        density = density_of(
            place,
            window,
            coeffs,
            [coeffs_x, coeffs_y],
            mixed,
            [weight_own, weight_oth],
            [vec_keep, vec_keep_c, vec_keep_x, vec_keep_xc],
            [
                ([keep], [same_a, same_b]),
                ([keep_c], [same_a_c, same_b_c]),
                ([cross], [diff_a, diff_b]),
                ([cross_c], [diff_a_c, diff_b_c]),
            ],
        )

    with jax.named_scope("subtract"):
        back, density = tie(back, density)
        out = subtract(eigvecs, back)
    return (out, density)


def cost(flops, bytes_accessed):
    return pl.CostEstimate(flops=flops, bytes_accessed=bytes_accessed, transcendentals=0)


def pack_kernel(n_tails, which, orbs, *refs):
    tails, out, orbs_v, out_v = refs[:n_tails], refs[n_tails], refs[n_tails + 1], refs[n_tails + 2]
    sems, tails_v = refs[-1], refs[n_tails + 3 : -1]
    parts, n_orbs, half = orbs_v.shape
    loads = []
    for i in range(parts):
        at = pl.ds(pl.multiple_of((2 * i + which[0]) * half, half), half)
        loads.append(pltpu.make_async_copy(orbs.at[:, at], orbs_v.at[i], sems.at[i]))
    for i, (tail, tail_v) in enumerate(zip(tails, tails_v)):
        loads.append(pltpu.make_async_copy(tail, tail_v, sems.at[parts + i]))
    for load in loads:
        load.start()
    for load in loads[parts:]:
        load.wait()
    stores = []
    for i in range(parts):
        loads[i].wait()
        out_v[i, :n_orbs, :] = orbs_v[i].astype(jnp.bfloat16)
        if n_tails == 2:
            for side in range(2):
                at = pl.ds((2 * i + side) * half, half)
                both = jnp.concatenate([tail_v[:, at] for tail_v in tails_v], axis=0)
                out_v[i, pl.ds(n_orbs + side * 16, 16), :] = both
        else:
            out_v[i, pl.ds(n_orbs, 16), :] = tails_v[0][...]
        if i % 4 == 3:
            at = pl.ds(i - 3, 4)
            sem = sems.at[parts + n_tails + i // 4]
            stores.append(pltpu.make_async_copy(out_v.at[at], out.at[at], sem))
            stores[-1].start()
    for store in stores:
        store.wait()


def pack(which, orbs, chunk, tails):
    n_orbs, n_basis = orbs.shape
    parts, half = n_basis // chunk, chunk // 2
    anywhere = pl.BlockSpec(memory_space=pl.ANY)
    shape = (parts, n_orbs + 16 * (2 if len(tails) == 2 else 1), half)
    return pl.pallas_call(
        functools.partial(pack_kernel, len(tails)),
        out_shape=jax.ShapeDtypeStruct(shape, jnp.bfloat16),
        in_specs=[pl.BlockSpec(memory_space=pltpu.SMEM)] + [anywhere] * (1 + len(tails)),
        out_specs=anywhere,
        scratch_shapes=[
            pltpu.VMEM((parts, n_orbs, half), jnp.float32),
            pltpu.VMEM(shape, jnp.bfloat16),
            *[pltpu.VMEM(tail.shape, jnp.bfloat16) for tail in tails],
            pltpu.SemaphoreType.DMA((parts + len(tails) + parts // 4,)),
        ],
        compiler_params=pltpu.CompilerParams(vmem_limit_bytes=62 * 2**20),
        cost_estimate=cost(0, 3 * n_orbs * n_basis),
        name="pack_vectors" if len(tails) == 2 else "pack_weights",
    )(which, orbs, *tails)


def subtract_kernel(orbs, update, out, orbs_v, update_v, sems):
    parts, _, chunk = update.shape
    step = parts // STEPS
    loads = []
    for i in range(STEPS):
        at, cols = pl.ds(i * step, step), pl.ds(i * step * chunk, step * chunk)
        loads.append(
            (
                pltpu.make_async_copy(update.at[at], update_v.at[at], sems.at[i]),
                pltpu.make_async_copy(orbs.at[:, cols], orbs_v.at[:, cols], sems.at[STEPS + i]),
            )
        )
        for load in loads[-1]:
            load.start()
    stores = []
    for i in range(STEPS):
        for load in loads[i]:
            load.wait()
        for part in range(i * step, (i + 1) * step):
            at = pl.ds(part * chunk, chunk)
            orbs_v[:, at] = orbs_v[:, at] - update_v[part].astype(jnp.float32)
        cols = pl.ds(i * step * chunk, step * chunk)
        sem = sems.at[2 * STEPS + i]
        stores.append(pltpu.make_async_copy(orbs_v.at[:, cols], out.at[:, cols], sem))
        stores[-1].start()
    for store in stores:
        store.wait()


def subtract(orbs, update):
    n_orbs, n_basis = orbs.shape
    anywhere = pl.BlockSpec(memory_space=pl.ANY)
    return pl.pallas_call(
        subtract_kernel,
        out_shape=jax.ShapeDtypeStruct(orbs.shape, jnp.float32),
        in_specs=[anywhere, anywhere],
        out_specs=anywhere,
        scratch_shapes=[
            pltpu.VMEM(orbs.shape, jnp.float32),
            pltpu.VMEM(update.shape, jnp.bfloat16),
            pltpu.SemaphoreType.DMA((3 * STEPS,)),
        ],
        compiler_params=pltpu.CompilerParams(vmem_limit_bytes=62 * 2**20),
        cost_estimate=cost(n_orbs * n_basis, 10 * n_orbs * n_basis),
        name="subtract_update",
    )(orbs, update)


def project_kernel(side, place, give, keep, vecs, vec_two, mine, theirs, kept, blocks_v, sems):
    blocks, n_own, lanes = mine.shape
    width = vecs.shape[1]
    n_rows, n_two = blocks * n_own, lanes - width
    stores = [pltpu.make_async_copy(keep.at[:, pl.ds(0, 2 * n_own)], kept, sems.at[2])]
    stores[0].start()
    for i, (out, half) in enumerate(((theirs, 1 - place[1]), (mine, place[1]))):
        at = pl.ds(pl.multiple_of(half * n_rows, n_rows), n_rows)
        proj = dot(give[at, :], vecs[1 - side[0]], ((1,), (1,)))
        rows = keep[pl.ds(half * (blocks // 2), blocks // 2), : 2 * n_own, :]
        rows = rows.reshape(n_rows, keep.shape[2])
        proj = proj + dot(rows, vecs[side[0]], ((1,), (1,)))
        blocks_v[i, :, :, :width] = proj.astype(jnp.bfloat16).reshape(blocks, n_own, width)
        at = pl.ds(pl.multiple_of(half * n_two, n_two), n_two)
        cross = dot(vecs[0], vec_two[0, at, :], ((1,), (1,)))
        cross = cross + dot(vecs[1], vec_two[1, at, :], ((1,), (1,)))
        blocks_v[i, :, :, width:] = cross.astype(jnp.bfloat16).reshape(blocks, n_own, n_two)
        stores.append(pltpu.make_async_copy(blocks_v.at[i], out, sems.at[i]))
        stores[-1].start()
    for store in stores:
        store.wait()


def specs_of(n_scalars, n_arrays):
    scalar = pl.BlockSpec(memory_space=pltpu.SMEM)
    return [scalar] * n_scalars + [pl.BlockSpec(memory_space=pltpu.VMEM)] * n_arrays


def project(side, place, give, keep, vecs, vec_two):
    shape = (16, give.shape[0] // 32, vecs.shape[1] + vec_two.shape[1] // 2)
    return pl.pallas_call(
        project_kernel,
        out_shape=(
            jax.ShapeDtypeStruct(shape, jnp.bfloat16),
            jax.ShapeDtypeStruct(shape, jnp.bfloat16),
            jax.ShapeDtypeStruct((16, 2 * shape[1], give.shape[1]), jnp.bfloat16),
        ),
        in_specs=specs_of(2, 4),
        out_specs=(pl.BlockSpec(memory_space=pltpu.HBM),) * 3,
        scratch_shapes=[
            pltpu.VMEM((2,) + shape, jnp.bfloat16),
            pltpu.SemaphoreType.DMA((3,)),
        ],
        compiler_params=pltpu.CompilerParams(vmem_limit_bytes=20 * 2**20),
        cost_estimate=cost(1, 1),
        name="project",
    )(side, place, give, keep, vecs, vec_two)


def expand_kernel(place, mine, theirs, wide_high, wide_low, vecs, *rest):
    coeffs, mixed, update, coeffs_v, mixed_v, update_v, sems = rest
    width, half = vecs.shape[1:]
    blocks, n_own, lanes = mine.shape
    lanes = lanes - width
    n_rows, n_parts, n_orbs = blocks * n_own, update.shape[0] // 2, update.shape[1]
    halves = ((place[1], mine), (1 - place[1], theirs))
    total = None
    for core, every in halves:
        cross = every[:, :, width:].reshape(width, lanes)
        for wide in (wide_high, wide_low):
            term = dot(cross, wide[core], ((1,), (0,)))
            total = term if total is None else total + term
    row = lax.broadcasted_iota(jnp.int32, total.shape, 0)
    first = jnp.bitwise_and(lax.shift_right_logical(row, 3), 1) == 0
    mixed_v[...] = jnp.where(first, total, 0.0).astype(jnp.bfloat16)
    stores = [pltpu.make_async_copy(mixed_v, mixed, sems.at[0])]
    stores[0].start()
    for i, (core, every) in enumerate(halves):
        base = every[:, :, :width].reshape(n_rows, width)
        fixed = base.astype(jnp.float32) - dot(base, mixed_v[...], ((1,), (0,)))
        fixed = fixed.astype(jnp.bfloat16)
        coeffs_v[i] = fixed
        for part in range(2):
            new = dot(fixed, vecs[part], ((1,), (0,))).astype(jnp.bfloat16)
            new = new.reshape(n_parts, n_orbs, half)
            update_v[i, :, :, part * half : (part + 1) * half] = new
        at = pl.ds(pl.multiple_of(core * n_rows, n_rows), n_rows)
        stores.append(pltpu.make_async_copy(coeffs_v.at[i], coeffs.at[at], sems.at[1 + i]))
        at = pl.ds(core * n_parts, n_parts)
        stores.append(pltpu.make_async_copy(update_v.at[i], update.at[at], sems.at[3 + i]))
        for store in stores[-2:]:
            store.start()
    for store in stores:
        store.wait()


def expand(place, mine, theirs, wide_high, wide_low, vecs, n_orbs):
    _, width, half = vecs.shape
    total = 2 * mine.shape[0] * mine.shape[1]
    wide_high, wide_low = (v.reshape(2, v.shape[0] // 2, width) for v in (wide_high, wide_low))
    return pl.pallas_call(
        expand_kernel,
        out_shape=(
            jax.ShapeDtypeStruct((total, width), jnp.bfloat16),
            jax.ShapeDtypeStruct((width, width), jnp.bfloat16),
            jax.ShapeDtypeStruct((16, n_orbs, 2 * half), jnp.bfloat16),
        ),
        in_specs=specs_of(1, 5),
        out_specs=(pl.BlockSpec(memory_space=pltpu.HBM),) * 3,
        scratch_shapes=[
            pltpu.VMEM((2, total // 2, width), jnp.bfloat16),
            pltpu.VMEM((width, width), jnp.bfloat16),
            pltpu.VMEM((2, 8, n_orbs, 2 * half), jnp.bfloat16),
            pltpu.SemaphoreType.DMA((5,)),
        ],
        compiler_params=pltpu.CompilerParams(vmem_limit_bytes=60 * 2**20 + 768 * 2**10),
        cost_estimate=cost(2 * total * width * (width + 2 * half), 6 * 2**20),
        name="expand",
    )(place, mine, theirs, wide_high, wide_low, vecs)


def density_kernel(counts, place, win_orbs, win_vecs, *refs):
    coeffs, coeffs_x, coeffs_y, mixed, weight_own, weight_oth = refs[:6]
    vecs, refs = refs[6:10], refs[10:]
    n_pieces = sum(counts)
    pieces, refs = refs[:n_pieces], refs[n_pieces:]
    out, orbs_v, vecs_v, coeffs_v, raw_v, mixed_v, weight_v, sems = refs
    n_half, width = coeffs.shape
    n_orbs, tile = n_half // 16, win_orbs.shape[2]

    @pl.when(pl.program_id(0) == 0)
    def _():
        copies = []

        def fetch(source, target):
            copy = pltpu.make_async_copy(source, target, sems.at[len(copies)])
            copy.start()
            copies.append(copy)
            return copy

        factors = [fetch(coeffs, coeffs_v.at[0]), fetch(mixed, mixed_v)]
        factors += [fetch(coeffs_x, raw_v.at[0]), fetch(coeffs_y, raw_v.at[1])]
        factors += [fetch(weight_own, weight_v.at[0]), fetch(weight_oth, weight_v.at[1])]
        sides, used = [], 0
        for side in range(4):
            needed = [fetch(vecs[side], vecs_v.at[side])]
            for part in range(2):
                n = counts[2 * side + part]
                for i in range(n):
                    at = pl.ds(i * (n_half // n), n_half // n)
                    needed.append(fetch(pieces[used + i], orbs_v.at[2 * side + part, at]))
                used += n
            sides.append(needed)

        for copy in factors:
            copy.wait()
        for i, core in enumerate((place[1], 1 - place[1])):
            raw = raw_v[i]
            fixed = raw.astype(jnp.float32) - dot(raw, mixed_v[...], ((1,), (0,)))
            to = pl.multiple_of(core * (n_half // 2), n_half // 2)
            coeffs_v[1, pl.ds(to, n_half // 2), :] = fixed.astype(jnp.bfloat16)
        for side in range(4):
            for copy in sides[side]:
                copy.wait()
            for part in range(2):
                slot = 2 * side + part
                update = dot(coeffs_v[part], vecs_v[side], ((1,), (0,)))
                new = (orbs_v[slot].astype(jnp.float32) - update) * weight_v[part]
                orbs_v[slot] = new.astype(jnp.bfloat16)

    vec_tile = win_vecs[...].reshape(width, tile)
    turned = []
    for part in range(2):
        update = dot(coeffs_v[part], vec_tile, ((1,), (0,)))
        value = win_orbs[:, part * n_orbs : (part + 1) * n_orbs, :].reshape(n_half, tile)
        turned.append((value.astype(jnp.float32) - update).astype(jnp.bfloat16).T)
    for block in range(4):
        side = jnp.bitwise_xor(place[0], block)
        total = dot(turned[0], orbs_v[2 * side], ((1,), (0,)))
        out[:, block, :] = total + dot(turned[1], orbs_v[2 * side + 1], ((1,), (0,)))


def density_of(place, window, coeffs, others, mixed, weights, vecs, orbs):
    rows = window.shape[2]
    n_half, width = coeffs.shape
    half = vecs[0].shape[1]
    n_vec, n_orbs = width // 16, n_half // 16
    counts = [len(part) for side in orbs for part in side]
    pieces = [piece for side in orbs for part in side for piece in part]
    operands = [coeffs, *others, mixed, *weights, *vecs, *pieces]
    specs = [
        pl.BlockSpec((16, 2 * n_orbs, TILE), lambda i, _: (0, 0, i)),
        pl.BlockSpec((16, n_vec, TILE), lambda i, _: (0, 2 * n_orbs // n_vec, i)),
    ]
    return pl.pallas_call(
        functools.partial(density_kernel, counts),
        out_shape=jax.ShapeDtypeStruct((rows, 4, half), jnp.float32),
        grid_spec=pltpu.PrefetchScalarGridSpec(
            num_scalar_prefetch=1,
            grid=(rows // TILE,),
            in_specs=specs + [pl.BlockSpec(memory_space=pl.ANY)] * len(operands),
            out_specs=pl.BlockSpec((TILE, 4, half), lambda i, _: (i, 0, 0)),
            scratch_shapes=[
                pltpu.VMEM((8, n_half, half), jnp.bfloat16),
                pltpu.VMEM((4, width, half), jnp.bfloat16),
                pltpu.VMEM((2, n_half, width), jnp.bfloat16),
                pltpu.VMEM((2, n_half // 2, width), jnp.bfloat16),
                pltpu.VMEM((width, width), jnp.bfloat16),
                pltpu.VMEM((2, n_half, 1), jnp.float32),
                pltpu.SemaphoreType.DMA((len(operands),)),
            ],
        ),
        compiler_params=pltpu.CompilerParams(vmem_limit_bytes=62 * 2**20),
        cost_estimate=cost(16 * rows * n_half * half + 16 * n_half * width * half, 28 * 2**20),
        name="density",
    )(place, window, window, *operands)


def solution(mesh):
    mesh = Mesh(mesh.devices.reshape(4, 4, 2, 2, 2), ("z", "y", "xl", "xh", "c"))
    slab, grid = ("z", "y", "xl"), ("xh", "c")
    both = P(slab, grid)
    in_specs = (both, both, both, P(), P(), P(slab), P(), P())
    out_specs = (both, P(grid, None, slab))
    return jax.shard_map(body, mesh=mesh, in_specs=in_specs, out_specs=out_specs, check_vma=False)
```
